128 devices in a mesh: inline: 8 (over z, core), xline: 16 (over x, y).
Axes of the slice: x: 4, y: 4, z: 4, core: 2. Of those that a mesh axis runs over, the one named last changes fastest.
Arguments:
- traces: bfloat16 [65536, 1536], P(('inline', 'xline')), may hold values from -6 to 6
- owner: int32 [65536, 1], P(('inline', 'xline')), may hold values from 0 to 127; in each aligned block of 512 rows (0 to 511, 512 to 1023, ...) at most 8 rows name the same one
- cell: int32 [65536], P(('inline', 'xline')), may hold values from 0 to 127
- shift_table: int32 [32, 1536], replicated, may hold values from 0 to 255, as said below
- weight_table: float32 [32, 1536], replicated, as said below
- gains: float32 [256], replicated, may hold values from 0.5 to 4
Outputs:
- filtered: float32 [1536, 64, 256], P('inline', 'xline')
The draws below stay inside these ranges and needn't reach their ends.
Inputs may be any that keep to these rules, and one draw needn't show every extreme that they name: owner is inline index * 16 + xline index of a device; among the 512 traces of one device no owner is named more than 8 times, a bound that some block reaches. `shift_table`: along t the shift of a class never rises; some class reaches 255 and some class reaches 0. `weight_table`: every entry is a whole number of 64ths, below 1.
All inputs are finite; a program needn't handle non-finite values.
Results may differ from the reference program's by a relative error of at most 0.0059.
Values may be sent and summed in bfloat16 or wider, within the bound.
No kernel may reach another device: no remote copies, remote signals or barrier semaphores. Data moves between devices by JAX's collectives and lax.ppermute only.
A program may use at most 128 MiB of HBM per device.

```python
import math
import jax
import jax.numpy as jnp
import numpy as np
from jax import lax

NT = 1536
TR_DEV = 512
BIL = 8
BXL = 16
NOFF = 32
SMAX = 256
TRACES = 65536
CAP = 8
NIL = 64
NXL = 256
N_XLINE = 16
DEVICES = 128


def moveout_tables(key):
    folded = jax.random.fold_in(key, 11)
    subkeys = jax.random.split(folded, 3)
    apex_values = jax.random.randint(subkeys[0], (NOFF,), 1, 2 * SMAX + 1)
    longest = jax.random.randint(subkeys[1], (), 0, NOFF)
    class_number = jnp.arange(NOFF, dtype=jnp.int32)
    apex_values = jnp.where(class_number == longest, 2 * SMAX, apex_values)
    apex_values = jnp.where(class_number == (longest + 1) % NOFF, 1, apex_values)
    growth = jax.random.randint(subkeys[2], (NOFF,), 1, 4)
    sample_times = jnp.arange(NT, dtype=jnp.int32)
    squared = (apex_values * apex_values * NT)[:, None] // (NT + growth[:, None] * sample_times[None, :])
    divisor = 2 * sample_times[None, :] + apex_values[:, None]
    integral = squared // divisor
    fraction = squared % divisor * 64 // divisor
    clamped = integral >= SMAX
    shifts = jnp.where(clamped, SMAX - 1, integral).astype(jnp.int32)
    weights = jnp.where(clamped, 0, fraction).astype(jnp.float32) / 64.0
    return (shifts, weights)


def draw_shift_table(key, part):
    return moveout_tables(key)[0]


def draw_weight_table(key, part):
    return moveout_tables(key)[1]


def set_ends(values, own_key, low, high):
    place = [jax.random.randint(jax.random.fold_in(own_key, axis), (), 0, length) for axis, length in enumerate(values.shape)]
    widest = values.shape.index(max(values.shape))
    neighbour = place[:widest] + [(place[widest] + 1) % values.shape[widest]] + place[widest + 1:]
    return values.at[tuple(place)].set(low).at[tuple(neighbour)].set(high)


def block_scale(key, dims, cuts, low, top_value):
    def one(dim, parts):
        heights = jax.random.uniform(jax.random.fold_in(jax.random.fold_in(key, 6), dim), (parts,), jnp.float32, low / len(cuts), top_value / len(cuts))
        return jnp.repeat(jnp.exp(heights), dims[dim] // parts).reshape((-1,) + (1,) * (len(dims) - dim - 1))

    factor_of = one(*cuts[0])
    for cut in cuts[1:]:
        factor_of = factor_of * one(*cut)
    return factor_of


def routed_block(key, own, number, rows, count, top, bound, skew):
    order = jax.random.permutation(key, count)
    packed, common = shares(count, rows * top, bound, skew, True), shares(count, rows * top, bound, skew, False)
    places = jnp.arange(count)

    def named(lengths, offset_by):
        used = int((lengths > 0).sum())
        fixed = max(1, used // 4)
        shifted = fixed + (places - fixed + offset_by * (used - fixed)) % max(1, count - fixed)
        return jnp.zeros((count,), jnp.int32).at[order[jnp.where(places < fixed, places, shifted)]].set(jnp.asarray(lengths, jnp.int32))

    lengths = jnp.where(number % 4 == 0, named(packed, number // 4), named(common, number - number // 4 - 1))
    mixed = jax.random.permutation(jax.random.fold_in(own, 3), count)
    giver, sink = mixed[0:count // 2 * 2:2], mixed[1:count // 2 * 2:2]
    room = jnp.minimum(lengths[giver] - 1, bound - lengths[sink]) // 2
    room = jnp.where((giver == order[0]) | (sink == order[0]) | (lengths[sink] == 0), 0, jnp.maximum(room, 0))
    shifted = jax.random.randint(jax.random.fold_in(own, 4), (count // 2,), 0, 1 << 20) % (room + 1)
    lengths = lengths.at[giver].add(-shifted).at[sink].add(shifted)
    labels = jnp.searchsorted(jnp.cumsum(lengths), jnp.arange(rows * top), side="right").astype(jnp.int32)
    table = labels.reshape(top, rows).T
    table = table[jax.random.permutation(jax.random.fold_in(own, 1), rows)]
    offset_by = jax.random.randint(jax.random.fold_in(own, 2), (rows, 1), 0, top)
    return jnp.take_along_axis(table, (jnp.arange(top)[None, :] + offset_by) % top, axis=1)


def shares(count, total, bound, skew, full):
    loads = [(1 << 20) // math.isqrt(grade ** skew) + 1 for grade in range(1, count + 1)]
    largest = bound if full else min(bound, max(-(-total // count), total * loads[0] // sum(loads)))
    least = 1 if total - largest >= count - 1 else 0
    counts, surplus = [largest] + [least] * (count - 1), total - largest - least * (count - 1)
    while surplus > 0:
        movable = [i for i in range(1, count) if counts[i] < largest] or [i for i in range(1, count) if counts[i] < bound]
        pool, left = sum([loads[i] for i in movable]), surplus
        for i in movable:
            addition = min(bound - counts[i], max(1, left * loads[i] // pool), surplus)
            counts[i] = counts[i] + addition
            surplus = surplus - addition
    return np.array(counts)


def scatter_about(stream_key, shape, width, bound, cuts=(), kind=jnp.bfloat16):
    gain = block_scale(stream_key, shape, cuts, -0.22, 0.18) if cuts else 1.0
    array = jax.random.normal(stream_key, shape, jnp.float32) * width * gain
    return jnp.minimum(jnp.maximum(array, -bound), bound).astype(kind)


def setup_inputs(seed: int = 0) -> dict:
    key_of = jax.random.split(jax.random.key(seed), 7)
    traces = scatter_about(key_of[0], (TRACES, NT), 1.0, 6.0, ((0, 128),))
    owner_keys = jax.random.split(jax.random.fold_in(key_of[1], 1), TRACES // TR_DEV)
    owner_turns = jax.random.permutation(jax.random.fold_in(key_of[1], 3), TRACES // TR_DEV)
    owner = jax.vmap(lambda own, number: routed_block(jax.random.fold_in(key_of[1], 2), own, number, TR_DEV, DEVICES, 1, CAP, 2))(owner_keys, owner_turns).reshape((TRACES, 1))
    cell = set_ends(jax.random.randint(key_of[2], (TRACES,), 0, BIL * BXL), jax.random.fold_in(key_of[2], 1), 0, (BIL * BXL) - 1).astype(jnp.int32)
    shift_table = draw_shift_table(jax.random.fold_in(key_of[6], 71), 0)
    weight_table = draw_weight_table(jax.random.fold_in(key_of[6], 71), 0)
    gains = jnp.clip(jnp.exp(jax.random.uniform(key_of[5], (NXL,), jnp.float32, math.log(0.5), math.log(4.0))), 0.5, 4.0)
    return dict(traces=traces, owner=owner, cell=cell, shift_table=shift_table, weight_table=weight_table, gains=gains)


def moveout(block, classes, shift_table, weight_table):
    shifts = jnp.take(shift_table, classes, axis=0)
    weights = jnp.take(weight_table, classes, axis=0)
    times = jnp.arange(NT, dtype=jnp.int32)[None, :] + shifts
    first = jnp.take_along_axis(block, jnp.clip(times, 0, NT - 1), axis=1).astype(jnp.float32)
    first = jnp.where(times < NT, first, 0.0)
    second = jnp.take_along_axis(block, jnp.clip(times + 1, 0, NT - 1), axis=1).astype(jnp.float32)
    second = jnp.where(times + 1 < NT, second, 0.0)
    return ((1.0 - weights) * first + weights * second).astype(jnp.bfloat16)


def crossline_filter(gains):
    count = gains.shape[0]
    index = jnp.arange(count, dtype=jnp.int32)
    phase = (index[:, None] * index[None, :]) % count
    table = jnp.cos(2.0 * jnp.pi * phase.astype(jnp.float32) / count)
    kernel = jnp.dot(table, gains, precision=lax.Precision.HIGHEST) / count
    spread = (index[:, None] - index[None, :]) % count
    return jnp.take(kernel, spread, axis=0).astype(jnp.bfloat16)


def reference(traces, owner, cell, shift_table, weight_table, gains):
    nbins = NIL * NXL
    dest = owner[:, 0]
    inline_bin = (dest // N_XLINE) * BIL + cell // BXL
    xline_bin = (dest % N_XLINE) * BXL + cell % BXL
    bins = (inline_bin * NXL + xline_bin).astype(jnp.int32)
    classes = (jnp.arange(TR_DEV, dtype=jnp.int32) // (TR_DEV // NOFF)).astype(jnp.int32)
    blocks = traces.reshape(DEVICES, TR_DEV, NT)

    def correct(block):
        return moveout(block, classes, shift_table, weight_table)

    moved = lax.map(correct, blocks).reshape(TRACES, NT)
    sums = jax.ops.segment_sum(moved.astype(jnp.float32), bins, num_segments=nbins)
    folds = jax.ops.segment_sum(jnp.ones((TRACES,), jnp.float32), bins, num_segments=nbins)
    stack = (sums / jnp.maximum(folds, 1.0)[:, None]).astype(jnp.bfloat16).reshape(NIL, NXL, NT)
    matrix = crossline_filter(gains)
    return jnp.einsum("ab,ibt->tia", matrix.astype(jnp.float32), stack.astype(jnp.float32))
```

```python
import functools

import numpy as np
import jax
import jax.numpy as jnp
from jax import lax
from jax.experimental import pallas as pl
from jax.experimental.pallas import tpu as pltpu
from jax.sharding import PartitionSpec as P

LANES = 128
ROWS = 512
SAMPLES = 1536
CLASSES = 32
GROUP = ROWS // CLASSES
TILES = SAMPLES // LANES
N_IN = 8
N_X = 16
DEVICES = N_IN * N_X
SLOTS = 64
HALF = LANES // 2
WHOLE = tuple(3 * (i // 2) + 2 * (i % 2) for i in range(N_IN))
SHARED = tuple(3 * i + 1 for i in range(N_IN // 2))
VMEM = 60 * 1024 * 1024


def iota(shape, dim):
    return lax.broadcasted_iota(jnp.int32, shape, dim)


def moveout(tiles, x_ref, shift_ref, weight_ref, moved_ref):
    lane = iota((8, LANES), 1)

    def eight_classes(e, carry):
        tables = pl.ds(pl.multiple_of(e * 8, 8), 8)
        shifts = [shift_ref[tables, k * LANES : (k + 1) * LANES] for k in tiles]
        weights = [weight_ref[tables, k * LANES : (k + 1) * LANES] for k in tiles]
        for c in range(8):
            one_class(pl.ds(pl.multiple_of(e * 8 * GROUP + c * GROUP, GROUP), GROUP), c, shifts, weights)
        return carry

    def one_class(rows, c, shifts, weights):
        halves = {}

        def source(k, h):
            if (k, 0) not in halves:
                both = x_ref[rows, k * LANES : (k + 1) * LANES].astype(jnp.float32)
                halves[k, 0], halves[k, 1] = both[:8], both[8:]
            return halves[k, h]

        for j, k in enumerate(tiles):
            shift = jnp.broadcast_to(shifts[j][c : c + 1], (8, LANES))
            weight = jnp.broadcast_to(weights[j][c : c + 1], (8, LANES))
            rest = 1.0 - weight
            parts = []
            early = lane + shift
            picks = []
            for u in (early, early + 1):
                picks.append((u & (LANES - 1), u < LANES, u < 2 * LANES))
            for h in range(2):
                values = []
                for index, in_first, in_second in picks:
                    got = [
                        jnp.take_along_axis(source(k + n, h), index, axis=1, mode="promise_in_bounds")
                        if k + n < TILES
                        else jnp.zeros((8, LANES), jnp.float32)
                        for n in range(3)
                    ]
                    values.append(jnp.where(in_first, got[0], jnp.where(in_second, got[1], got[2])))
                parts.append(rest * values[0] + weight * values[1])
            moved_ref[rows, j * LANES : (j + 1) * LANES] = jnp.concatenate(parts, axis=0).astype(
                jnp.bfloat16
            )

    lax.fori_loop(0, CLASSES // 8, eight_classes, 0)


def slot_of_rows(owner_row):
    owners = owner_row.astype(jnp.float32)
    blocks = [owners[:, b * LANES : (b + 1) * LANES] for b in range(ROWS // LANES)]
    columns = [jnp.transpose(jnp.broadcast_to(b, (LANES, LANES))) for b in blocks]
    earlier = iota((LANES, LANES), 0) < iota((LANES, LANES), 1)
    ranks = []
    for b, block in enumerate(blocks):
        total = jnp.zeros((LANES, LANES), jnp.float32)
        for a in range(b + 1):
            same = columns[a] == block
            if a == b:
                same = same & earlier
            total = total + jnp.where(same, 1.0, 0.0)
        ranks.append(jnp.sum(total, axis=0, keepdims=True))
    rank = jnp.concatenate(ranks, axis=1).astype(jnp.int32)
    return (owner_row & (N_X - 1)) * SLOTS + (owner_row >> 4) * 8 + rank


def spread(slot, place_ref):
    for m in range(N_X * SLOTS // LANES):
        here = iota((LANES, ROWS), 0) + m * LANES == slot
        place_ref[m * LANES : (m + 1) * LANES, :] = jnp.where(here, 1.0, 0.0).astype(jnp.bfloat16)


def pack_whole_kernel(owner_ref, cell_ref, shift_ref, weight_ref, x_ref, out_ref, slot_ref, moved_ref, place_ref):
    slot = slot_of_rows(owner_ref[...])
    slot_ref[...] = slot
    spread(slot, place_ref)
    code = ((slot >> 3) & 1) * LANES + cell_ref[...] + 1
    line = (slot >> 6) * 8 + ((slot >> 4) & 3)
    held = jnp.where(iota((LANES, ROWS), 0) == line, code.astype(jnp.float32), 0.0).astype(jnp.bfloat16)
    lanes = jnp.where((iota((LANES, ROWS), 0) & 15) == (slot & 15), 1.0, 0.0).astype(jnp.bfloat16)
    codes = lax.dot_general(
        held, lanes, (((1,), (1,)), ((), ())), preferred_element_type=jnp.float32
    ).astype(jnp.bfloat16)
    for x in range(N_X):
        for i in range(N_IN):
            out_ref[i * N_X + x, SLOTS : SLOTS + 8, :] = codes[x * 8 : (x + 1) * 8]
    moveout(WHOLE, x_ref, shift_ref, weight_ref, moved_ref)

    def two_groups(m, carry):
        place = place_ref[pl.ds(pl.multiple_of(m * LANES, LANES), LANES), :]
        for n in range(0, N_IN, 2):
            result = jnp.dot(
                place, moved_ref[:, n * LANES : (n + 2) * LANES], preferred_element_type=jnp.float32
            ).astype(jnp.bfloat16)
            for i in range(n, n + 2):
                for x in range(2):
                    out_ref[i * N_X + 2 * m + x, 0:SLOTS, :] = result[
                        x * SLOTS : (x + 1) * SLOTS, (i - n) * LANES : (i - n + 1) * LANES
                    ]
        return carry

    lax.fori_loop(0, N_X // 2, two_groups, 0)


def pack_shared_kernel(slot_ref, shift_ref, weight_ref, x_ref, out_ref, moved_ref, place_ref):
    spread(slot_ref[...], place_ref)
    moveout(SHARED, x_ref, shift_ref, weight_ref, moved_ref)
    low = iota((SLOTS // 2, LANES), 1) < HALF

    def two_groups(m, carry):
        place = place_ref[pl.ds(pl.multiple_of(m * LANES, LANES), LANES), :]
        for n in range(0, len(SHARED), 2):
            result = jnp.dot(
                place, moved_ref[:, n * LANES : (n + 2) * LANES], preferred_element_type=jnp.float32
            )
            for k in range(n, n + 2):
                for x in range(2):
                    block = result[x * SLOTS : (x + 1) * SLOTS, (k - n) * LANES : (k - n + 1) * LANES]
                    first, second = block[: SLOTS // 2], block[SLOTS // 2 :]
                    even = jnp.where(low, first, pltpu.roll(second, HALF, 1))
                    odd = jnp.where(low, pltpu.roll(first, HALF, 1), second)
                    out_ref[2 * k * N_X + 2 * m + x] = even.astype(jnp.bfloat16)
                    out_ref[(2 * k + 1) * N_X + 2 * m + x] = odd.astype(jnp.bfloat16)
        return carry

    lax.fori_loop(0, N_X // 2, two_groups, 0)


def stack_kernel(whole_ref, shared_ref, out_ref, select_ref):
    bins = (iota((2 * LANES, LANES), 0) + 1).astype(jnp.float32).astype(jnp.bfloat16)
    depth = DEVICES * 16
    ones = jnp.ones((depth, LANES), jnp.bfloat16)
    lines = []
    for j in range(DEVICES // 8):
        line = jnp.zeros((8, LANES), jnp.float32)
        for g in range(8):
            mine = (iota((8, LANES), 1) >> 4) == g
            codes = whole_ref[8 * j + g, SLOTS : SLOTS + 8, :].astype(jnp.float32)
            line = jnp.where(mine, codes, line)
        lines.append(line)
    low = iota((32, LANES), 1) < HALF
    for p in range(4):
        for j in range(DEVICES // 8):
            row = jnp.broadcast_to(lines[j][p : p + 1], (16, LANES)).astype(jnp.bfloat16)
            row = jnp.concatenate([row] * 16, axis=0)
            select_ref[:, j * LANES : (j + 1) * LANES] = jnp.where(
                bins == row, jnp.bfloat16(1), jnp.bfloat16(0)
            )
        select = select_ref[...]
        full = whole_ref[:, 16 * p : 16 * p + 16, :].reshape(depth, LANES)
        q = p % 2
        half = shared_ref[:, 16 * q : 16 * q + 16, :].reshape(depth, LANES)
        sums = jnp.dot(select, jnp.concatenate([full, ones], axis=1), preferred_element_type=jnp.float32)
        fold = jnp.maximum(sums[:, LANES:], 1.0)
        mean = sums[:, :LANES] / fold
        part = jnp.dot(select, half, preferred_element_type=jnp.float32) / fold
        for x in range(4):
            rows = slice(64 * x, 64 * x + 64)
            out_ref[4 * p + x, 0:64, :] = mean[rows].astype(jnp.bfloat16)
            first, second = part[64 * x : 64 * x + 32], part[64 * x + 32 : 64 * x + 64]
            if p < 2:
                packed = jnp.where(low, first, pltpu.roll(second, HALF, 1))
            else:
                packed = jnp.where(low, pltpu.roll(first, HALF, 1), second)
            out_ref[4 * p + x, 64:96, :] = packed.astype(jnp.bfloat16)


def filter_kernel(order_ref, matrix_ref, slab_ref, out_ref):
    whole_at, shared_at = order_ref[0], order_ref[1]
    matrix = matrix_ref[...]
    count = N_X * 16

    def apply(block):
        return lax.dot_general(block, matrix, (((0,), (0,)), ((), ())), preferred_element_type=jnp.float32)

    for i in range(4):
        full = slab_ref[:, 16 * i : 16 * i + 16, :].reshape(count, LANES)
        out_ref[pl.ds(whole_at, LANES), i, :] = apply(full)
    for i in range(2):
        pair = slab_ref[:, 64 + 16 * i : 80 + 16 * i, :].reshape(count, LANES)
        both = apply(pair)
        out_ref[pl.ds(shared_at, HALF), i, :] = both[:HALF]
        out_ref[pl.ds(shared_at, HALF), i + 2, :] = both[HALF:]


def call(kernel, name, out_shape, scratch, in_specs=None):
    extra = {} if in_specs is None else {"in_specs": in_specs}
    return pl.pallas_call(
        kernel,
        out_shape=out_shape,
        scratch_shapes=scratch,
        name=name,
        compiler_params=pltpu.CompilerParams(vmem_limit_bytes=VMEM),
        **extra,
    )


def crossline_filter(gains):
    count = gains.shape[0]
    index = np.arange(count)
    phase = 2.0 * np.pi * (index[:, None] * index[None, :] % count) / count
    basis = np.concatenate([np.cos(phase), np.sin(phase)], axis=1).astype(np.float32)
    scaled = basis * jnp.concatenate([gains, gains])[None, :]
    dims = (((1,), (1,)), ((), ()))
    product = lax.dot_general(scaled, jnp.asarray(basis), dims, precision=lax.Precision.HIGHEST)
    return (product / count).astype(jnp.bfloat16)


def exchange(block, axes):
    return lax.all_to_all(block, axes, split_axis=0, concat_axis=0, tiled=True)


def shards(traces, owner, cell, shift_table, weight_table, gains):
    bf16, both = jnp.bfloat16, ("inline", "xline")
    owner_row, cell_row = owner.reshape(1, ROWS), cell.reshape(1, ROWS)
    place = pltpu.VMEM((N_X * SLOTS, ROWS), bf16)
    whole, slot = call(
        pack_whole_kernel,
        "pack_whole",
        (
            jax.ShapeDtypeStruct((DEVICES, SLOTS + 8, LANES), bf16),
            jax.ShapeDtypeStruct((1, ROWS), jnp.int32),
        ),
        [pltpu.VMEM((ROWS, len(WHOLE) * LANES), bf16), place],
    )(owner_row, cell_row, shift_table, weight_table, traces)
    whole = exchange(whole, both)
    shared = call(
        pack_shared_kernel,
        "pack_shared",
        jax.ShapeDtypeStruct((DEVICES, SLOTS // 2, LANES), bf16),
        [pltpu.VMEM((ROWS, len(SHARED) * LANES), bf16), place],
    )(slot, shift_table, weight_table, traces)
    shared = exchange(shared, both)
    matrix = crossline_filter(gains)
    stacked = call(
        stack_kernel,
        "stack",
        jax.ShapeDtypeStruct((N_X, 96, LANES), bf16),
        [pltpu.VMEM((2 * LANES, DEVICES * 16), bf16)],
    )(whole, shared)
    slab = exchange(stacked, "xline")
    odd = lax.axis_index("inline") % 2
    order = jnp.stack([odd * HALF, (1 - odd) * LANES])
    vmem = pl.BlockSpec(memory_space=pltpu.VMEM)
    return call(
        filter_kernel,
        "crossline",
        jax.ShapeDtypeStruct((SAMPLES // N_IN, 4, N_X * 16), jnp.float32),
        [],
        [pl.BlockSpec(memory_space=pltpu.SMEM), vmem, vmem],
    )(order, matrix, slab)


def solution(mesh):
    split = P(("inline", "xline"))
    placed = (P(("inline", "xline"), None), P(("inline", "xline"), None), split, P(), P(), P())
    return jax.shard_map(
        shards, mesh=mesh, in_specs=placed, out_specs=P("inline", "xline", None), check_vma=False
    )
```

```python
import functools

import numpy as np
import jax
import jax.numpy as jnp
from jax import lax
from jax.experimental import pallas as pl
from jax.experimental.pallas import tpu as pltpu
from jax.sharding import PartitionSpec as P

LANES = 128
ROWS = 512
SAMPLES = 1536
CLASSES = 32
GROUP = ROWS // CLASSES
TILES = SAMPLES // LANES
N_IN = 8
N_X = 16
DEVICES = N_IN * N_X
SLOTS = 64
HALF = LANES // 2
CODES = SLOTS + SLOTS // 2
MIB = 1024 * 1024


def iota(shape, dim):
    return lax.broadcasted_iota(jnp.int32, shape, dim)


def narrow_windows(shift_ref):
    lane = iota((CLASSES, LANES), 1)
    widest = jnp.zeros((CLASSES, 1), jnp.float32)
    for k in range(TILES):
        u = (lane + shift_ref[:, k * LANES : (k + 1) * LANES]).astype(jnp.float32)
        widest = jnp.maximum(widest, jnp.max(u, axis=1, keepdims=True) - jnp.min(u, axis=1, keepdims=True))
    return jnp.max(widest) < LANES


def moveout(narrow, rows_ready, x_ref, shift_ref, weight_ref, moved_ref):
    lane = iota((8, LANES), 1)

    def lanes_of(values, index):
        return jnp.take_along_axis(values, index, axis=1, mode="promise_in_bounds")

    def first_below(u, sources):
        chosen = sources[2]
        for n in (1, 0):
            if sources[n] is not chosen:
                chosen = jnp.where(u < (n + 1) * LANES, sources[n], chosen)
        return chosen

    def one_tile(e, narrow, k, shifts, weights):
        places = lane + shifts
        lowest = jnp.min(places.astype(jnp.float32), axis=1, keepdims=True).astype(jnp.int32)
        lowest = jnp.broadcast_to(lowest, (8, LANES))
        for c in range(8):
            rows = pl.ds(pl.multiple_of(e * 8 * GROUP + c * GROUP, GROUP), GROUP)
            early = jnp.broadcast_to(places[c : c + 1], (8, LANES))
            weight = jnp.broadcast_to(weights[c : c + 1], (8, LANES))
            rest = 1.0 - weight
            blank = jnp.zeros((8, LANES), jnp.float32)
            halves = [[], []]
            for n in range(3):
                if k + n < TILES:
                    both = x_ref[rows, (k + n) * LANES : (k + n + 1) * LANES].astype(jnp.float32)
                    halves[0].append(both[:8])
                    halves[1].append(both[8:])
                else:
                    halves[0].append(blank)
                    halves[1].append(blank)
            picks = []
            if narrow:
                low = jnp.broadcast_to(lowest[c : c + 1], (8, LANES))
                for step in range(2):
                    held = low + step + ((lane - low - step) & (LANES - 1))
                    picks.append(((early + step) & (LANES - 1), held))
            parts = []
            for sources in halves:
                if narrow:
                    values = [lanes_of(first_below(held, sources), index) for index, held in picks]
                else:
                    values = []
                    for step in range(2):
                        u = early + step
                        index = u & (LANES - 1)
                        got = [s if s is blank else lanes_of(s, index) for s in sources]
                        values.append(first_below(u, got))
                parts.append(rest * values[0] + weight * values[1])
            moved_ref[rows, k * LANES : (k + 1) * LANES] = jnp.concatenate(parts, axis=0).astype(jnp.bfloat16)

    def eight_classes(narrow, e):
        tables = pl.ds(pl.multiple_of(e * 8, 8), 8)
        for k in range(TILES):
            at = slice(k * LANES, (k + 1) * LANES)
            one_tile(e, narrow, k, shift_ref[tables, at], weight_ref[tables, at])

    def step(e, carry):
        rows_ready(e)

        @pl.when(narrow)
        def _():
            eight_classes(True, e)

        @pl.when(jnp.logical_not(narrow))
        def _():
            eight_classes(False, e)

        return carry

    lax.fori_loop(0, CLASSES // 8, step, 0)


def slot_of_rows(owner_row):
    owners = owner_row.astype(jnp.float32)
    blocks = [owners[:, b * LANES : (b + 1) * LANES] for b in range(ROWS // LANES)]
    columns = [jnp.transpose(jnp.broadcast_to(b, (LANES, LANES))) for b in blocks]
    earlier = iota((LANES, LANES), 0) < iota((LANES, LANES), 1)
    ranks = []
    for b, block in enumerate(blocks):
        total = jnp.zeros((LANES, LANES), jnp.float32)
        for a in range(b + 1):
            same = columns[a] == block
            if a == b:
                same = same & earlier
            total = total + jnp.where(same, 1.0, 0.0)
        ranks.append(jnp.sum(total, axis=0, keepdims=True))
    rank = jnp.concatenate(ranks, axis=1).astype(jnp.int32)
    return (owner_row & (N_X - 1)) * SLOTS + (owner_row >> 4) * 8 + rank


def spread(slot, place_ref):
    for m in range(N_X * SLOTS // LANES):
        here = iota((LANES, ROWS), 0) + m * LANES == slot
        place_ref[m * LANES : (m + 1) * LANES, :] = jnp.where(here, 1.0, 0.0).astype(jnp.bfloat16)


def pack_kernel(
    owner_hbm, cell_hbm, shift_hbm, weight_hbm, x_hbm, out_hbm,
    owner_ref, cell_ref, shift_ref, weight_ref, x_ref, moved_ref, place_ref, out_ref, small_sem, in_sem, out_sem,
):
    quarter = ROWS // 4
    small = [
        pltpu.make_async_copy(source, target, small_sem.at[n])
        for n, (source, target) in enumerate(
            [(owner_hbm, owner_ref), (cell_hbm, cell_ref), (shift_hbm, shift_ref), (weight_hbm, weight_ref)]
        )
    ]
    for copy in small:
        copy.start()

    def arrival(e):
        rows = pl.ds(pl.multiple_of(e * quarter, quarter), quarter)
        return pltpu.make_async_copy(x_hbm.at[rows], x_ref.at[rows], in_sem.at[e])

    def departure(m):
        groups = pl.ds(2 * m, 2)
        return pltpu.make_async_copy(out_ref.at[:, groups], out_hbm.at[:, groups], out_sem.at[m])

    for e in range(4):
        arrival(e).start()
    small[0].wait()
    slot = slot_of_rows(owner_ref[...])
    spread(slot, place_ref)
    small[1].wait()
    code = ((slot >> 3) & 1) * LANES + cell_ref[...] + 1
    line = (slot >> 6) * 8 + ((slot >> 4) & 3)
    held = jnp.where(iota((LANES, ROWS), 0) == line, code.astype(jnp.float32), 0.0).astype(jnp.bfloat16)
    lanes = jnp.where((iota((LANES, ROWS), 0) & 15) == (slot & 15), 1.0, 0.0).astype(jnp.bfloat16)
    codes = lax.dot_general(
        held, lanes, (((1,), (1,)), ((), ())), preferred_element_type=jnp.float32
    ).astype(jnp.bfloat16)
    for x in range(N_X):
        for i in range(N_IN):
            out_ref[i, x, CODES : CODES + 8, :] = codes[x * 8 : (x + 1) * 8]
    small[2].wait()
    small[3].wait()
    moveout(
        narrow_windows(shift_ref), lambda e: arrival(e).wait(), x_ref, shift_ref, weight_ref, moved_ref
    )
    low = iota((SLOTS // 2, LANES), 1) < HALF

    def two_groups(m, carry):
        place = place_ref[pl.ds(pl.multiple_of(m * LANES, LANES), LANES), :]
        for n in range(N_IN // 2):
            result = jnp.dot(
                place, moved_ref[:, 3 * n * LANES : 3 * (n + 1) * LANES], preferred_element_type=jnp.float32
            )
            for x in range(2):
                block = result[x * SLOTS : (x + 1) * SLOTS]
                out_ref[2 * n, 2 * m + x, 0:SLOTS, :] = block[:, :LANES].astype(jnp.bfloat16)
                out_ref[2 * n + 1, 2 * m + x, 0:SLOTS, :] = block[:, 2 * LANES :].astype(jnp.bfloat16)
                middle = block[:, LANES : 2 * LANES]
                first, second = middle[: SLOTS // 2], middle[SLOTS // 2 :]
                even = jnp.where(low, first, pltpu.roll(second, HALF, 1))
                odd = jnp.where(low, pltpu.roll(first, HALF, 1), second)
                out_ref[2 * n, 2 * m + x, SLOTS:CODES, :] = even.astype(jnp.bfloat16)
                out_ref[2 * n + 1, 2 * m + x, SLOTS:CODES, :] = odd.astype(jnp.bfloat16)
        departure(m).start()
        return carry

    lax.fori_loop(0, N_X // 2, two_groups, 0)
    for m in range(N_X // 2):
        departure(m).wait()


def stack_kernel(slots_ref, out_hbm, select_ref, out_ref, out_sem):
    bins = (iota((2 * LANES, LANES), 0) + 1).astype(jnp.float32).astype(jnp.bfloat16)
    depth = DEVICES * 16
    ones = jnp.ones((depth, LANES), jnp.bfloat16)
    lines = []
    for j in range(DEVICES // 8):
        line = jnp.zeros((8, LANES), jnp.float32)
        for g in range(8):
            mine = (iota((8, LANES), 1) >> 4) == g
            codes = slots_ref[8 * j + g, CODES : CODES + 8, :].astype(jnp.float32)
            line = jnp.where(mine, codes, line)
        lines.append(line)
    low = iota((32, LANES), 1) < HALF

    def departure(p):
        return pltpu.make_async_copy(out_ref.at[4 * p : 4 * p + 4], out_hbm.at[4 * p : 4 * p + 4], out_sem.at[p])

    for p in range(4):
        for j in range(DEVICES // 8):
            row = jnp.broadcast_to(lines[j][p : p + 1], (16, LANES)).astype(jnp.bfloat16)
            row = jnp.concatenate([row] * 16, axis=0)
            select_ref[:, j * LANES : (j + 1) * LANES] = jnp.where(
                bins == row, jnp.bfloat16(1), jnp.bfloat16(0)
            )
        select = select_ref[...]
        full = slots_ref[:, 16 * p : 16 * p + 16, :].reshape(depth, LANES)
        q = p % 2
        half = slots_ref[:, SLOTS + 16 * q : SLOTS + 16 * q + 16, :].reshape(depth, LANES)
        sums = jnp.dot(select, jnp.concatenate([full, ones], axis=1), preferred_element_type=jnp.float32)
        fold = jnp.maximum(sums[:, LANES:], 1.0)
        mean = sums[:, :LANES] / fold
        part = jnp.dot(select, half, preferred_element_type=jnp.float32) / fold
        for x in range(4):
            rows = slice(64 * x, 64 * x + 64)
            out_ref[4 * p + x, 0:64, :] = mean[rows].astype(jnp.bfloat16)
            first, second = part[64 * x : 64 * x + 32], part[64 * x + 32 : 64 * x + 64]
            if p < 2:
                packed = jnp.where(low, first, pltpu.roll(second, HALF, 1))
            else:
                packed = jnp.where(low, pltpu.roll(first, HALF, 1), second)
            out_ref[4 * p + x, 64:96, :] = packed.astype(jnp.bfloat16)
        departure(p).start()
    for p in range(4):
        departure(p).wait()


def filter_kernel(order_ref, matrix_ref, slab_ref, out_ref):
    whole_at, shared_at = order_ref[0], order_ref[1]
    matrix = matrix_ref[...]
    count = N_X * 16

    def apply(block):
        return lax.dot_general(block, matrix, (((0,), (0,)), ((), ())), preferred_element_type=jnp.float32)

    for i in range(4):
        full = slab_ref[:, 16 * i : 16 * i + 16, :].reshape(count, LANES)
        out_ref[pl.ds(whole_at, LANES), i, :] = apply(full)
    for i in range(2):
        pair = slab_ref[:, 64 + 16 * i : 80 + 16 * i, :].reshape(count, LANES)
        both = apply(pair)
        out_ref[pl.ds(shared_at, HALF), i, :] = both[:HALF]
        out_ref[pl.ds(shared_at, HALF), i + 2, :] = both[HALF:]


def call(kernel, name, out_shape, scratch, in_specs, out_specs, mib):
    return pl.pallas_call(
        kernel,
        out_shape=out_shape,
        scratch_shapes=scratch,
        name=name,
        in_specs=in_specs,
        out_specs=out_specs,
        compiler_params=pltpu.CompilerParams(vmem_limit_bytes=mib * MIB),
    )


def crossline_filter(gains):
    count = gains.shape[0]
    index = np.arange(count)
    phase = 2.0 * np.pi * (index[:, None] * index[None, :] % count) / count
    basis = np.concatenate([np.cos(phase), np.sin(phase)], axis=1).astype(np.float32)
    scaled = basis * jnp.concatenate([gains, gains])[None, :]
    dims = (((1,), (1,)), ((), ()))
    product = lax.dot_general(scaled, jnp.asarray(basis), dims, precision=lax.Precision.HIGHEST)
    return (product / count).astype(jnp.bfloat16)


def exchange(block, axes):
    return lax.all_to_all(block, axes, split_axis=0, concat_axis=0, tiled=True)


def shards(traces, owner, cell, shift_table, weight_table, gains):
    bf16, dma = jnp.bfloat16, pltpu.SemaphoreType.DMA
    vmem, smem = pl.BlockSpec(memory_space=pltpu.VMEM), pl.BlockSpec(memory_space=pltpu.SMEM)
    hbm = pl.BlockSpec(memory_space=pltpu.HBM)
    owner_row, cell_row = owner.reshape(1, ROWS), cell.reshape(1, ROWS)
    out = (N_IN, N_X, CODES + 8, LANES)
    slots = call(
        pack_kernel,
        "pack",
        jax.ShapeDtypeStruct(out, bf16),
        [
            pltpu.VMEM((1, ROWS), jnp.int32),
            pltpu.VMEM((1, ROWS), jnp.int32),
            pltpu.VMEM((CLASSES, SAMPLES), jnp.int32),
            pltpu.VMEM((CLASSES, SAMPLES), jnp.float32),
            pltpu.VMEM((ROWS, SAMPLES), bf16),
            pltpu.VMEM((ROWS, SAMPLES), bf16),
            pltpu.VMEM((N_X * SLOTS, ROWS), bf16),
            pltpu.VMEM(out, bf16),
            dma((4,)),
            dma((4,)),
            dma((N_X // 2,)),
        ],
        [hbm] * 5,
        hbm,
        60,
    )(owner_row, cell_row, shift_table, weight_table, traces)
    slots = exchange(slots.reshape(DEVICES, CODES + 8, LANES), ("inline", "xline"))
    matrix = crossline_filter(gains)
    stacked = call(
        stack_kernel,
        "stack",
        jax.ShapeDtypeStruct((N_X, 96, LANES), bf16),
        [pltpu.VMEM((2 * LANES, DEVICES * 16), bf16), pltpu.VMEM((N_X, 96, LANES), bf16), dma((4,))],
        [vmem],
        hbm,
        32,
    )(slots)
    slab = exchange(stacked, "xline")
    odd = lax.axis_index("inline") % 2
    order = jnp.stack([odd * HALF, (1 - odd) * LANES])
    return call(
        filter_kernel,
        "crossline",
        jax.ShapeDtypeStruct((SAMPLES // N_IN, 4, N_X * 16), jnp.float32),
        [],
        [smem, vmem, vmem],
        vmem,
        16,
    )(order, matrix, slab)


def solution(mesh):
    split = P(("inline", "xline"))
    placed = (P(("inline", "xline"), None), P(("inline", "xline"), None), split, P(), P(), P())
    return jax.shard_map(
        shards, mesh=mesh, in_specs=placed, out_specs=P("inline", "xline", None), check_vma=False
    )
```

```python
import functools

import numpy as np
import jax
import jax.numpy as jnp
from jax import lax
from jax.experimental import pallas as pl
from jax.experimental.pallas import tpu as pltpu
from jax.sharding import PartitionSpec as P

LANES = 128
ROWS = 512
SAMPLES = 1536
CLASSES = 32
GROUP = ROWS // CLASSES
TILES = SAMPLES // LANES
N_IN = 8
N_X = 16
DEVICES = N_IN * N_X
SLOTS = 64
HALF = LANES // 2
CODES = SLOTS + SLOTS // 2
MIB = 1024 * 1024


def iota(shape, dim):
    return lax.broadcasted_iota(jnp.int32, shape, dim)


def table_places(shift_ref, places_ref):
    lane = iota((8, LANES), 1)
    widest = jnp.zeros((8, 1), jnp.float32)
    for e in range(CLASSES // 8):
        rows = slice(8 * e, 8 * e + 8)
        for k in range(TILES):
            at = slice(k * LANES, (k + 1) * LANES)
            u = lane + shift_ref[rows, at]
            low = jnp.min(u.astype(jnp.float32), axis=1, keepdims=True)
            high = jnp.max(u.astype(jnp.float32), axis=1, keepdims=True)
            widest = jnp.maximum(widest, high - low)
            low = jnp.broadcast_to(low.astype(jnp.int32), (8, LANES))
            for step in range(2):
                places_ref[step, rows, at] = (u + step) & (LANES - 1)
                places_ref[2 + step, rows, at] = low + step + ((lane - low - step) & (LANES - 1))
    return jnp.max(widest) < LANES


def lanes_of(values, index):
    return jnp.take_along_axis(values, index, axis=1, mode="promise_in_bounds")


def first_below(u, sources):
    chosen = sources[2]
    for n in (1, 0):
        if sources[n] is not chosen:
            chosen = jnp.where(u < (n + 1) * LANES, sources[n], chosen)
    return chosen


def moveout(narrow, k, c, row_of, rows, x_ref, shift_ref, weight_ref, places_ref, moved_ref):
    at = slice(k * LANES, (k + 1) * LANES)
    weight = row_of(weight_ref, c, at)
    rest = 1.0 - weight
    blank = jnp.zeros((8, LANES), jnp.float32)
    halves = [[], []]
    for n in range(3):
        both = None
        if k + n < TILES:
            both = x_ref[rows, (k + n) * LANES : (k + n + 1) * LANES].astype(jnp.float32)
        halves[0].append(blank if both is None else both[:8])
        halves[1].append(blank if both is None else both[8:])
    parts = [[], []]
    for step in range(2):
        if narrow:
            index, held = row_of(places_ref.at[step], c, at), row_of(places_ref.at[2 + step], c, at)
            for h, sources in enumerate(halves):
                parts[h].append(lanes_of(first_below(held, sources), index))
        else:
            u = iota((8, LANES), 1) + row_of(shift_ref, c, at) + step
            for h, sources in enumerate(halves):
                got = [s if s is blank else lanes_of(s, u & (LANES - 1)) for s in sources]
                parts[h].append(first_below(u, got))
    mixed = [rest * first + weight * second for first, second in parts]
    moved_ref[rows, at] = jnp.concatenate(mixed, axis=0).astype(jnp.bfloat16)


def slot_of_rows(owner_row):
    owners = owner_row.astype(jnp.float32)
    blocks = [owners[:, b * LANES : (b + 1) * LANES] for b in range(ROWS // LANES)]
    columns = [jnp.transpose(jnp.broadcast_to(b, (LANES, LANES))) for b in blocks]
    earlier = iota((LANES, LANES), 0) < iota((LANES, LANES), 1)
    ranks = []
    for b, block in enumerate(blocks):
        total = jnp.zeros((LANES, LANES), jnp.float32)
        for a in range(b + 1):
            same = columns[a] == block
            if a == b:
                same = same & earlier
            total = total + jnp.where(same, 1.0, 0.0)
        ranks.append(jnp.sum(total, axis=0, keepdims=True))
    rank = jnp.concatenate(ranks, axis=1).astype(jnp.int32)
    return (owner_row & (N_X - 1)) * SLOTS + (owner_row >> 4) * 8 + rank


def spread(slot, place_ref):
    for m in range(N_X * SLOTS // LANES):
        here = iota((LANES, ROWS), 0) + m * LANES == slot
        place_ref[m * LANES : (m + 1) * LANES, :] = jnp.where(here, 1.0, 0.0).astype(jnp.bfloat16)


def pack_kernel(
    owner_hbm, cell_hbm, shift_hbm, weight_hbm, x_hbm, out_hbm,
    owner_ref, cell_ref, shift_ref, weight_ref, x_ref, places_ref, moved_ref, place_ref, out_ref, in_sem, out_sem,
):
    arrays = [
        (owner_hbm, owner_ref), (cell_hbm, cell_ref), (shift_hbm, shift_ref), (weight_hbm, weight_ref), (x_hbm, x_ref),
    ]
    arrivals = [pltpu.make_async_copy(a, b, in_sem.at[n]) for n, (a, b) in enumerate(arrays)]
    departures = [pltpu.make_async_copy(out_ref.at[i], out_hbm.at[i], out_sem.at[i]) for i in range(N_IN)]
    for copy in arrivals:
        copy.start()
    arrivals[0].wait()
    slot = slot_of_rows(owner_ref[...])
    spread(slot, place_ref)
    arrivals[1].wait()
    code = ((slot >> 3) & 1) * LANES + cell_ref[...] + 1
    line = (slot >> 6) * 8 + ((slot >> 4) & 3)
    held = jnp.where(iota((LANES, ROWS), 0) == line, code.astype(jnp.float32), 0.0).astype(jnp.bfloat16)
    lanes = jnp.where((iota((LANES, ROWS), 0) & 15) == (slot & 15), 1.0, 0.0).astype(jnp.bfloat16)
    codes = lax.dot_general(
        held, lanes, (((1,), (1,)), ((), ())), preferred_element_type=jnp.float32
    ).astype(jnp.bfloat16)
    for x in range(N_X):
        for i in range(N_IN):
            out_ref[i, x, CODES : CODES + 8, :] = codes[x * 8 : (x + 1) * 8]
    for copy in arrivals[2:]:
        copy.wait()
    low = iota((SLOTS // 2, LANES), 1) < HALF

    def place_pair(n):
        result = jnp.dot(
            place_ref[...], moved_ref[:, 2 * n * LANES : 2 * (n + 1) * LANES], preferred_element_type=jnp.float32
        )
        for k in (2 * n, 2 * n + 1):
            even = 2 * (k // 3)
            for x in range(N_X):
                block = result[x * SLOTS : (x + 1) * SLOTS, (k - 2 * n) * LANES : (k - 2 * n + 1) * LANES]
                if k % 3 != 1:
                    out_ref[even + k % 3 // 2, x, 0:SLOTS, :] = block.astype(jnp.bfloat16)
                    continue
                first, second = block[: SLOTS // 2], block[SLOTS // 2 :]
                out_ref[even, x, SLOTS:CODES, :] = jnp.where(
                    low, first, pltpu.roll(second, HALF, 1)
                ).astype(jnp.bfloat16)
                out_ref[even + 1, x, SLOTS:CODES, :] = jnp.where(
                    low, pltpu.roll(first, HALF, 1), second
                ).astype(jnp.bfloat16)
            if k % 3:
                departures[even + k % 3 - 1].start()

    def all_tiles(narrow):
        refs = x_ref, shift_ref, weight_ref, places_ref, moved_ref

        if narrow:
            for n in range(TILES // 2 + 1):
                if n < TILES // 2:
                    for k in (2 * n, 2 * n + 1):
                        for c in range(CLASSES):
                            moveout(
                                True, k, c,
                                lambda ref, c, at: jnp.broadcast_to(ref[c : c + 1, at], (8, LANES)),
                                slice(c * GROUP, (c + 1) * GROUP), *refs,
                            )
                if n:
                    place_pair(n - 1)
            return

        def step(e, carry):
            tables = pl.ds(pl.multiple_of(e * 8, 8), 8)
            for c in range(8):
                rows = pl.ds(pl.multiple_of(e * 8 * GROUP + c * GROUP, GROUP), GROUP)
                for k in range(TILES):
                    moveout(
                        False, k, c,
                        lambda ref, c, at: jnp.broadcast_to(ref[tables, at][c : c + 1], (8, LANES)),
                        rows, *refs,
                    )
            return carry

        lax.fori_loop(0, CLASSES // 8, step, 0)
        for n in range(TILES // 2):
            place_pair(n)

    narrow = table_places(shift_ref, places_ref)
    pl.when(narrow)(lambda: all_tiles(True))
    pl.when(jnp.logical_not(narrow))(lambda: all_tiles(False))
    for copy in departures:
        copy.wait()


def stack_kernel(slots_ref, out_hbm, select_ref, out_ref, out_sem):
    bins = (iota((2 * LANES, LANES), 0) + 1).astype(jnp.float32).astype(jnp.bfloat16)
    depth = DEVICES * 16
    ones = jnp.ones((depth, LANES), jnp.bfloat16)
    lines = []
    for j in range(DEVICES // 8):
        line = jnp.zeros((8, LANES), jnp.float32)
        for g in range(8):
            mine = (iota((8, LANES), 1) >> 4) == g
            codes = slots_ref[8 * j + g, CODES : CODES + 8, :].astype(jnp.float32)
            line = jnp.where(mine, codes, line)
        lines.append(line)
    low = iota((32, LANES), 1) < HALF

    def departure(p):
        return pltpu.make_async_copy(out_ref.at[4 * p : 4 * p + 4], out_hbm.at[4 * p : 4 * p + 4], out_sem.at[p])

    for p in range(4):
        for j in range(DEVICES // 8):
            row = jnp.broadcast_to(lines[j][p : p + 1], (16, LANES)).astype(jnp.bfloat16)
            row = jnp.concatenate([row] * 16, axis=0)
            select_ref[:, j * LANES : (j + 1) * LANES] = jnp.where(
                bins == row, jnp.bfloat16(1), jnp.bfloat16(0)
            )
        select = select_ref[...]
        full = slots_ref[:, 16 * p : 16 * p + 16, :].reshape(depth, LANES)
        q = p % 2
        half = slots_ref[:, SLOTS + 16 * q : SLOTS + 16 * q + 16, :].reshape(depth, LANES)
        sums = jnp.dot(select, jnp.concatenate([full, ones], axis=1), preferred_element_type=jnp.float32)
        fold = jnp.maximum(sums[:, LANES:], 1.0)
        mean = sums[:, :LANES] / fold
        part = jnp.dot(select, half, preferred_element_type=jnp.float32) / fold
        for x in range(4):
            rows = slice(64 * x, 64 * x + 64)
            out_ref[4 * p + x, 0:64, :] = mean[rows].astype(jnp.bfloat16)
            first, second = part[64 * x : 64 * x + 32], part[64 * x + 32 : 64 * x + 64]
            if p < 2:
                packed = jnp.where(low, first, pltpu.roll(second, HALF, 1))
            else:
                packed = jnp.where(low, pltpu.roll(first, HALF, 1), second)
            out_ref[4 * p + x, 64:96, :] = packed.astype(jnp.bfloat16)
        departure(p).start()
    for p in range(4):
        departure(p).wait()


def filter_kernel(order_ref, matrix_ref, slab_ref, out_ref):
    whole_at, shared_at = order_ref[0], order_ref[1]
    matrix = matrix_ref[...]
    count = N_X * 16

    def apply(block):
        return lax.dot_general(block, matrix, (((0,), (0,)), ((), ())), preferred_element_type=jnp.float32)

    for i in range(4):
        full = slab_ref[:, 16 * i : 16 * i + 16, :].reshape(count, LANES)
        out_ref[pl.ds(whole_at, LANES), i, :] = apply(full)
    for i in range(2):
        pair = slab_ref[:, 64 + 16 * i : 80 + 16 * i, :].reshape(count, LANES)
        both = apply(pair)
        out_ref[pl.ds(shared_at, HALF), i, :] = both[:HALF]
        out_ref[pl.ds(shared_at, HALF), i + 2, :] = both[HALF:]


def call(kernel, name, out_shape, scratch, in_specs, out_specs, mib):
    return pl.pallas_call(
        kernel,
        out_shape=out_shape,
        scratch_shapes=scratch,
        name=name,
        in_specs=in_specs,
        out_specs=out_specs,
        compiler_params=pltpu.CompilerParams(vmem_limit_bytes=mib * MIB),
    )


def crossline_filter(gains):
    count = gains.shape[0]
    index = np.arange(count)
    phase = 2.0 * np.pi * (index[:, None] * index[None, :] % count) / count
    basis = np.concatenate([np.cos(phase), np.sin(phase)], axis=1).astype(np.float32)
    scaled = basis * jnp.concatenate([gains, gains])[None, :]
    dims = (((1,), (1,)), ((), ()))
    product = lax.dot_general(scaled, jnp.asarray(basis), dims, precision=lax.Precision.HIGHEST)
    return (product / count).astype(jnp.bfloat16)


def exchange(block, axes):
    return lax.all_to_all(block, axes, split_axis=0, concat_axis=0, tiled=True)


def shards(traces, owner, cell, shift_table, weight_table, gains):
    bf16, dma = jnp.bfloat16, pltpu.SemaphoreType.DMA
    vmem, smem = pl.BlockSpec(memory_space=pltpu.VMEM), pl.BlockSpec(memory_space=pltpu.SMEM)
    hbm = pl.BlockSpec(memory_space=pltpu.HBM)
    owner_row, cell_row = owner.reshape(1, ROWS), cell.reshape(1, ROWS)
    out = (N_IN, N_X, CODES + 8, LANES)
    slots = call(
        pack_kernel,
        "pack",
        jax.ShapeDtypeStruct(out, bf16),
        [
            pltpu.VMEM((1, ROWS), jnp.int32),
            pltpu.VMEM((1, ROWS), jnp.int32),
            pltpu.VMEM((CLASSES, SAMPLES), jnp.int32),
            pltpu.VMEM((CLASSES, SAMPLES), jnp.float32),
            pltpu.VMEM((ROWS, SAMPLES), bf16),
            pltpu.VMEM((4, CLASSES, SAMPLES), jnp.int32),
            pltpu.VMEM((ROWS, SAMPLES), bf16),
            pltpu.VMEM((N_X * SLOTS, ROWS), bf16),
            pltpu.VMEM(out, bf16),
            dma((5,)),
            dma((N_IN,)),
        ],
        [hbm] * 5,
        hbm,
        60,
    )(owner_row, cell_row, shift_table, weight_table, traces)
    slots = exchange(slots.reshape(DEVICES, CODES + 8, LANES), ("inline", "xline"))
    matrix = crossline_filter(gains)
    stacked = call(
        stack_kernel,
        "stack",
        jax.ShapeDtypeStruct((N_X, 96, LANES), bf16),
        [pltpu.VMEM((2 * LANES, DEVICES * 16), bf16), pltpu.VMEM((N_X, 96, LANES), bf16), dma((4,))],
        [vmem],
        hbm,
        32,
    )(slots)
    slab = exchange(stacked, "xline")
    odd = lax.axis_index("inline") % 2
    order = jnp.stack([odd * HALF, (1 - odd) * LANES])
    return call(
        filter_kernel,
        "crossline",
        jax.ShapeDtypeStruct((SAMPLES // N_IN, 4, N_X * 16), jnp.float32),
        [],
        [smem, vmem, vmem],
        vmem,
        16,
    )(order, matrix, slab)


def solution(mesh):
    split = P(("inline", "xline"))
    placed = (P(("inline", "xline"), None), P(("inline", "xline"), None), split, P(), P(), P())
    return jax.shard_map(
        shards, mesh=mesh, in_specs=placed, out_specs=P("inline", "xline", None), check_vma=False
    )
```

```python
import functools

import numpy as np
import jax
import jax.numpy as jnp
from jax import lax
from jax.experimental import pallas as pl
from jax.experimental.pallas import tpu as pltpu
from jax.sharding import PartitionSpec as P

LANES = 128
ROWS = 512
SAMPLES = 1536
CLASSES = 32
GROUP = ROWS // CLASSES
TILES = SAMPLES // LANES
N_IN = 8
N_X = 16
DEVICES = N_IN * N_X
SLOTS = 64
HALF = LANES // 2
CODES = SLOTS + SLOTS // 2
MIB = 1024 * 1024


def iota(shape, dim):
    return lax.broadcasted_iota(jnp.int32, shape, dim)


def table_places(shift_ref, places_ref):
    lane = iota((8, LANES), 1)
    widest = jnp.zeros((8, 1), jnp.float32)
    for e in range(CLASSES // 8):
        rows = slice(8 * e, 8 * e + 8)
        for k in range(TILES):
            at = slice(k * LANES, (k + 1) * LANES)
            u = lane + shift_ref[rows, at]
            low = jnp.min(u.astype(jnp.float32), axis=1, keepdims=True)
            high = jnp.max(u.astype(jnp.float32), axis=1, keepdims=True)
            widest = jnp.maximum(widest, high - low)
            low = jnp.broadcast_to(low.astype(jnp.int32), (8, LANES))
            for step in range(2):
                places_ref[step, rows, at] = (u + step) & (LANES - 1)
                places_ref[2 + step, rows, at] = low + step + ((lane - low - step) & (LANES - 1))
    return jnp.max(widest) < LANES


def lanes_of(values, index):
    return jnp.take_along_axis(values, index, axis=1, mode="promise_in_bounds")


def first_below(u, sources):
    chosen = sources[2]
    for n in (1, 0):
        if sources[n] is not chosen:
            chosen = jnp.where(u < (n + 1) * LANES, sources[n], chosen)
    return chosen


def moveout(narrow, k, c, row_of, rows, x_ref, shift_ref, weight_ref, places_ref, moved_ref):
    at = slice(k * LANES, (k + 1) * LANES)
    weight = row_of(weight_ref, c, at)
    rest = 1.0 - weight
    blank = jnp.zeros((8, LANES), jnp.float32)
    halves = [[], []]
    for n in range(3):
        both = None
        if k + n < TILES:
            both = x_ref[rows, (k + n) * LANES : (k + n + 1) * LANES].astype(jnp.float32)
        halves[0].append(blank if both is None else both[:8])
        halves[1].append(blank if both is None else both[8:])
    parts = [[], []]
    for step in range(2):
        if narrow:
            index, held = row_of(places_ref.at[step], c, at), row_of(places_ref.at[2 + step], c, at)
            for h, sources in enumerate(halves):
                parts[h].append(lanes_of(first_below(held, sources), index))
        else:
            u = iota((8, LANES), 1) + row_of(shift_ref, c, at) + step
            for h, sources in enumerate(halves):
                got = [s if s is blank else lanes_of(s, u & (LANES - 1)) for s in sources]
                parts[h].append(first_below(u, got))
    mixed = [rest * first + weight * second for first, second in parts]
    moved_ref[rows, at] = jnp.concatenate(mixed, axis=0).astype(jnp.bfloat16)


def slot_of_rows(owner_row):
    owners = owner_row.astype(jnp.float32)
    blocks = [owners[:, b * LANES : (b + 1) * LANES] for b in range(ROWS // LANES)]
    columns = [jnp.transpose(jnp.broadcast_to(b, (LANES, LANES))) for b in blocks]
    earlier = iota((LANES, LANES), 0) < iota((LANES, LANES), 1)
    ranks = []
    for b, block in enumerate(blocks):
        total = jnp.zeros((LANES, LANES), jnp.float32)
        for a in range(b + 1):
            same = columns[a] == block
            if a == b:
                same = same & earlier
            total = total + jnp.where(same, 1.0, 0.0)
        ranks.append(jnp.sum(total, axis=0, keepdims=True))
    rank = jnp.concatenate(ranks, axis=1).astype(jnp.int32)
    return (owner_row & (N_X - 1)) * SLOTS + (owner_row >> 4) * 8 + rank


def spread(slot, place_ref):
    for m in range(N_X * SLOTS // LANES):
        here = iota((LANES, ROWS), 0) + m * LANES == slot
        place_ref[m * LANES : (m + 1) * LANES, :] = jnp.where(here, 1.0, 0.0).astype(jnp.bfloat16)


def filter_basis():
    count = N_X * 16
    index = np.arange(count)
    phase = 2.0 * np.pi * (index[:, None] * index[None, :] % count) / count
    return np.concatenate([np.cos(phase), np.sin(phase)], axis=1).astype(np.float32)


def crossline_filter(gains, basis):
    count = basis.shape[0]
    scaled = basis * jnp.concatenate([gains, gains], axis=1)
    dims = (((1,), (1,)), ((), ()))
    product = lax.dot_general(
        scaled, basis, dims, precision=lax.Precision.HIGHEST, preferred_element_type=jnp.float32
    )
    return (product / count).astype(jnp.bfloat16)


def pack_kernel(
    owner_hbm, cell_hbm, gains_hbm, basis_hbm, shift_hbm, weight_hbm, x_hbm, out_hbm, matrix_hbm,
    owner_ref, cell_ref, gains_ref, basis_ref, shift_ref, weight_ref, x_ref, matrix_ref, places_ref, moved_ref, place_ref, out_ref, in_sem, out_sem,
):
    arrays = [
        (owner_hbm, owner_ref), (cell_hbm, cell_ref), (shift_hbm, shift_ref), (weight_hbm, weight_ref), (x_hbm, x_ref),
        (gains_hbm, gains_ref), (basis_hbm, basis_ref),
    ]
    arrivals = [pltpu.make_async_copy(a, b, in_sem.at[n]) for n, (a, b) in enumerate(arrays)]
    departures = [pltpu.make_async_copy(out_ref.at[i], out_hbm.at[i], out_sem.at[i]) for i in range(N_IN)]
    departures.append(pltpu.make_async_copy(matrix_ref, matrix_hbm, out_sem.at[N_IN]))
    for copy in arrivals:
        copy.start()
    arrivals[0].wait()
    slot = slot_of_rows(owner_ref[...])
    spread(slot, place_ref)
    arrivals[1].wait()
    code = ((slot >> 3) & 1) * LANES + cell_ref[...] + 1
    line = (slot >> 6) * 8 + ((slot >> 4) & 3)
    held = jnp.where(iota((LANES, ROWS), 0) == line, code.astype(jnp.float32), 0.0).astype(jnp.bfloat16)
    lanes = jnp.where((iota((LANES, ROWS), 0) & 15) == (slot & 15), 1.0, 0.0).astype(jnp.bfloat16)
    codes = lax.dot_general(
        held, lanes, (((1,), (1,)), ((), ())), preferred_element_type=jnp.float32
    ).astype(jnp.bfloat16)
    for x in range(N_X):
        for i in range(N_IN):
            out_ref[i, x, CODES : CODES + 8, :] = codes[x * 8 : (x + 1) * 8]
    for copy in arrivals[2:]:
        copy.wait()
    matrix_ref[...] = crossline_filter(gains_ref[...], basis_ref[...])
    departures[N_IN].start()
    low = iota((SLOTS // 2, LANES), 1) < HALF

    def place_pair(n):
        result = jnp.dot(
            place_ref[...], moved_ref[:, 2 * n * LANES : 2 * (n + 1) * LANES], preferred_element_type=jnp.float32
        )
        for k in (2 * n, 2 * n + 1):
            even = 2 * (k // 3)
            for x in range(N_X):
                block = result[x * SLOTS : (x + 1) * SLOTS, (k - 2 * n) * LANES : (k - 2 * n + 1) * LANES]
                if k % 3 != 1:
                    out_ref[even + k % 3 // 2, x, 0:SLOTS, :] = block.astype(jnp.bfloat16)
                    continue
                first, second = block[: SLOTS // 2], block[SLOTS // 2 :]
                out_ref[even, x, SLOTS:CODES, :] = jnp.where(
                    low, first, pltpu.roll(second, HALF, 1)
                ).astype(jnp.bfloat16)
                out_ref[even + 1, x, SLOTS:CODES, :] = jnp.where(
                    low, pltpu.roll(first, HALF, 1), second
                ).astype(jnp.bfloat16)
            if k % 3:
                departures[even + k % 3 - 1].start()

    def all_tiles(narrow):
        refs = x_ref, shift_ref, weight_ref, places_ref, moved_ref

        if narrow:
            for n in range(TILES // 2 + 1):
                if n < TILES // 2:
                    for k in (2 * n, 2 * n + 1):
                        for c in range(CLASSES):
                            moveout(
                                True, k, c,
                                lambda ref, c, at: jnp.broadcast_to(ref[c : c + 1, at], (8, LANES)),
                                slice(c * GROUP, (c + 1) * GROUP), *refs,
                            )
                if n:
                    place_pair(n - 1)
            return

        def step(e, carry):
            tables = pl.ds(pl.multiple_of(e * 8, 8), 8)
            for c in range(8):
                rows = pl.ds(pl.multiple_of(e * 8 * GROUP + c * GROUP, GROUP), GROUP)
                for k in range(TILES):
                    moveout(
                        False, k, c,
                        lambda ref, c, at: jnp.broadcast_to(ref[tables, at][c : c + 1], (8, LANES)),
                        rows, *refs,
                    )
            return carry

        lax.fori_loop(0, CLASSES // 8, step, 0)
        for n in range(TILES // 2):
            place_pair(n)

    narrow = table_places(shift_ref, places_ref)
    pl.when(narrow)(lambda: all_tiles(True))
    pl.when(jnp.logical_not(narrow))(lambda: all_tiles(False))
    for copy in departures:
        copy.wait()


def stack_kernel(slots_ref, out_hbm, select_ref, out_ref, out_sem):
    bins = (iota((2 * LANES, LANES), 0) + 1).astype(jnp.float32).astype(jnp.bfloat16)
    depth = DEVICES * 16
    ones = jnp.ones((depth, LANES), jnp.bfloat16)
    lines = []
    for j in range(DEVICES // 8):
        line = jnp.zeros((8, LANES), jnp.float32)
        for g in range(8):
            mine = (iota((8, LANES), 1) >> 4) == g
            codes = slots_ref[8 * j + g, CODES : CODES + 8, :].astype(jnp.float32)
            line = jnp.where(mine, codes, line)
        lines.append(line)
    low = iota((32, LANES), 1) < HALF

    def departure(p):
        return pltpu.make_async_copy(out_ref.at[4 * p : 4 * p + 4], out_hbm.at[4 * p : 4 * p + 4], out_sem.at[p])

    for p in range(4):
        for j in range(DEVICES // 8):
            row = jnp.broadcast_to(lines[j][p : p + 1], (16, LANES)).astype(jnp.bfloat16)
            row = jnp.concatenate([row] * 16, axis=0)
            select_ref[:, j * LANES : (j + 1) * LANES] = jnp.where(
                bins == row, jnp.bfloat16(1), jnp.bfloat16(0)
            )
        select = select_ref[...]
        full = slots_ref[:, 16 * p : 16 * p + 16, :].reshape(depth, LANES)
        q = p % 2
        half = slots_ref[:, SLOTS + 16 * q : SLOTS + 16 * q + 16, :].reshape(depth, LANES)
        sums = jnp.dot(select, jnp.concatenate([full, ones], axis=1), preferred_element_type=jnp.float32)
        fold = jnp.maximum(sums[:, LANES:], 1.0)
        mean = sums[:, :LANES] / fold
        part = jnp.dot(select, half, preferred_element_type=jnp.float32) / fold
        for x in range(4):
            rows = slice(64 * x, 64 * x + 64)
            out_ref[4 * p + x, 0:64, :] = mean[rows].astype(jnp.bfloat16)
            first, second = part[64 * x : 64 * x + 32], part[64 * x + 32 : 64 * x + 64]
            if p < 2:
                packed = jnp.where(low, first, pltpu.roll(second, HALF, 1))
            else:
                packed = jnp.where(low, pltpu.roll(first, HALF, 1), second)
            out_ref[4 * p + x, 64:96, :] = packed.astype(jnp.bfloat16)
        departure(p).start()
    for p in range(4):
        departure(p).wait()


def filter_kernel(matrix_ref, slab_ref, out_ref):
    odd = lax.axis_index("inline") & 1
    whole_at, shared_at = odd * HALF, (1 - odd) * LANES
    matrix = matrix_ref[...]
    count = N_X * 16

    def apply(block):
        return lax.dot_general(block, matrix, (((0,), (0,)), ((), ())), preferred_element_type=jnp.float32)

    for i in range(4):
        full = slab_ref[:, 16 * i : 16 * i + 16, :].reshape(count, LANES)
        out_ref[pl.ds(whole_at, LANES), i, :] = apply(full)
    for i in range(2):
        pair = slab_ref[:, 64 + 16 * i : 80 + 16 * i, :].reshape(count, LANES)
        both = apply(pair)
        out_ref[pl.ds(shared_at, HALF), i, :] = both[:HALF]
        out_ref[pl.ds(shared_at, HALF), i + 2, :] = both[HALF:]


def call(kernel, name, out_shape, scratch, in_specs, out_specs, mib):
    return pl.pallas_call(
        kernel,
        out_shape=out_shape,
        scratch_shapes=scratch,
        name=name,
        in_specs=in_specs,
        out_specs=out_specs,
        compiler_params=pltpu.CompilerParams(vmem_limit_bytes=mib * MIB),
    )


def exchange(block, axes):
    return lax.all_to_all(block, axes, split_axis=0, concat_axis=0, tiled=True)


def shards(traces, owner, cell, shift_table, weight_table, gains):
    bf16, dma = jnp.bfloat16, pltpu.SemaphoreType.DMA
    vmem = pl.BlockSpec(memory_space=pltpu.VMEM)
    hbm = pl.BlockSpec(memory_space=pltpu.HBM)
    owner_row, cell_row = owner.reshape(1, ROWS), cell.reshape(1, ROWS)
    out = (N_IN, N_X, CODES + 8, LANES)
    count = N_X * 16
    slots, matrix = call(
        pack_kernel,
        "pack",
        (jax.ShapeDtypeStruct(out, bf16), jax.ShapeDtypeStruct((count, count), bf16)),
        [
            pltpu.VMEM((1, ROWS), jnp.int32),
            pltpu.VMEM((1, ROWS), jnp.int32),
            pltpu.VMEM((1, count), jnp.float32),
            pltpu.VMEM((count, 2 * count), jnp.float32),
            pltpu.VMEM((CLASSES, SAMPLES), jnp.int32),
            pltpu.VMEM((CLASSES, SAMPLES), jnp.float32),
            pltpu.VMEM((ROWS, SAMPLES), bf16),
            pltpu.VMEM((count, count), bf16),
            pltpu.VMEM((4, CLASSES, SAMPLES), jnp.int32),
            pltpu.VMEM((ROWS, SAMPLES), bf16),
            pltpu.VMEM((N_X * SLOTS, ROWS), bf16),
            pltpu.VMEM(out, bf16),
            dma((7,)),
            dma((N_IN + 1,)),
        ],
        [hbm] * 7,
        (hbm, hbm),
        60,
    )(owner_row, cell_row, gains.reshape(1, count), jnp.asarray(filter_basis()), shift_table, weight_table, traces)
    slots = exchange(slots.reshape(DEVICES, CODES + 8, LANES), ("inline", "xline"))
    stacked = call(
        stack_kernel,
        "stack",
        jax.ShapeDtypeStruct((N_X, 96, LANES), bf16),
        [pltpu.VMEM((2 * LANES, DEVICES * 16), bf16), pltpu.VMEM((N_X, 96, LANES), bf16), dma((4,))],
        [vmem],
        hbm,
        32,
    )(slots)
    slab = exchange(stacked, "xline")
    return call(
        filter_kernel,
        "crossline",
        jax.ShapeDtypeStruct((SAMPLES // N_IN, 4, N_X * 16), jnp.float32),
        [],
        [vmem, vmem],
        vmem,
        16,
    )(matrix, slab)


def solution(mesh):
    split = P(("inline", "xline"))
    placed = (P(("inline", "xline"), None), P(("inline", "xline"), None), split, P(), P(), P())
    return jax.shard_map(
        shards, mesh=mesh, in_specs=placed, out_specs=P("inline", "xline", None), check_vma=False
    )
```

```python
import functools

import numpy as np
import jax
import jax.numpy as jnp
from jax import lax
from jax.experimental import pallas as pl
from jax.experimental.pallas import tpu as pltpu
from jax.sharding import PartitionSpec as P

LANES = 128
ROWS = 512
SAMPLES = 1536
CLASSES = 32
GROUP = ROWS // CLASSES
TILES = SAMPLES // LANES
N_IN = 8
N_X = 16
DEVICES = N_IN * N_X
SLOTS = 128
CHUNK = 32
CODES = 96
MIB = 1024 * 1024


def iota(shape, dim):
    return lax.broadcasted_iota(jnp.int32, shape, dim)


def table_places(shift_ref, places_ref):
    lane = iota((8, LANES), 1)
    widest = jnp.zeros((8, 1), jnp.float32)
    for e in range(CLASSES // 8):
        rows = slice(8 * e, 8 * e + 8)
        for k in range(TILES):
            at = slice(k * LANES, (k + 1) * LANES)
            u = lane + shift_ref[rows, at]
            low = jnp.min(u.astype(jnp.float32), axis=1, keepdims=True)
            high = jnp.max(u.astype(jnp.float32), axis=1, keepdims=True)
            widest = jnp.maximum(widest, high - low)
            low = jnp.broadcast_to(low.astype(jnp.int32), (8, LANES))
            for step in range(2):
                places_ref[step, rows, at] = (u + step) & (LANES - 1)
                places_ref[2 + step, rows, at] = low + step + ((lane - low - step) & (LANES - 1))
    return jnp.max(widest) < LANES


def lanes_of(values, index):
    return jnp.take_along_axis(values, index, axis=1, mode="promise_in_bounds")


def first_below(u, sources):
    chosen = sources[2]
    for n in (1, 0):
        if sources[n] is not chosen:
            chosen = jnp.where(u < (n + 1) * LANES, sources[n], chosen)
    return chosen


def moveout(narrow, k, c, row_of, rows, x_ref, shift_ref, weight_ref, places_ref, moved_ref):
    at = slice(k * LANES, (k + 1) * LANES)
    weight = row_of(weight_ref, c, at)
    rest = 1.0 - weight
    blank = jnp.zeros((8, LANES), jnp.float32)
    halves = [[], []]
    for n in range(3):
        both = None
        if k + n < TILES:
            both = x_ref[rows, (k + n) * LANES : (k + n + 1) * LANES].astype(jnp.float32)
        halves[0].append(blank if both is None else both[:8])
        halves[1].append(blank if both is None else both[8:])
    parts = [[], []]
    for step in range(2):
        if narrow:
            index, held = row_of(places_ref.at[step], c, at), row_of(places_ref.at[2 + step], c, at)
            for h, sources in enumerate(halves):
                parts[h].append(lanes_of(first_below(held, sources), index))
        else:
            u = iota((8, LANES), 1) + row_of(shift_ref, c, at) + step
            for h, sources in enumerate(halves):
                got = [s if s is blank else lanes_of(s, u & (LANES - 1)) for s in sources]
                parts[h].append(first_below(u, got))
    mixed = [rest * first + weight * second for first, second in parts]
    moved_ref[rows, at] = jnp.concatenate(mixed, axis=0).astype(jnp.bfloat16)


def slot_of_rows(owner_row):
    owners = owner_row.astype(jnp.float32)
    blocks = [owners[:, b * LANES : (b + 1) * LANES] for b in range(ROWS // LANES)]
    columns = [jnp.transpose(jnp.broadcast_to(b, (LANES, LANES))) for b in blocks]
    earlier = iota((LANES, LANES), 0) < iota((LANES, LANES), 1)
    ranks = []
    for b, block in enumerate(blocks):
        total = jnp.zeros((LANES, LANES), jnp.float32)
        for a in range(b + 1):
            same = columns[a] == block
            if a == b:
                same = same & earlier
            total = total + jnp.where(same, 1.0, 0.0)
        ranks.append(jnp.sum(total, axis=0, keepdims=True))
    rank = jnp.concatenate(ranks, axis=1).astype(jnp.int32)
    return owner_row * 8 + rank


def spread(slot, place_ref):
    for m in range(N_IN * SLOTS // LANES):
        here = iota((LANES, ROWS), 0) + m * LANES == slot
        place_ref[m * LANES : (m + 1) * LANES, :] = jnp.where(here, 1.0, 0.0).astype(jnp.bfloat16)


def filter_basis():
    count = N_X * 16
    index = np.arange(count)
    phase = 2.0 * np.pi * (index[:, None] * index[None, :] % count) / count
    return np.concatenate([np.cos(phase), np.sin(phase)], axis=1).astype(np.float32)


def crossline_filter(gains, basis):
    count = basis.shape[0]
    scaled = basis * jnp.concatenate([gains, gains], axis=1)
    dims = (((1,), (1,)), ((), ()))
    product = lax.dot_general(
        scaled, basis, dims, precision=lax.Precision.HIGHEST, preferred_element_type=jnp.float32
    )
    return (product / count).astype(jnp.bfloat16)


def pack_kernel(
    owner_hbm, cell_hbm, gains_hbm, basis_hbm, shift_hbm, weight_hbm, x_hbm, out_hbm, matrix_hbm,
    owner_ref, cell_ref, gains_ref, basis_ref, shift_ref, weight_ref, x_ref, matrix_ref, places_ref, moved_ref, place_ref, out_ref, in_sem, out_sem,
):
    arrays = [
        (owner_hbm, owner_ref), (cell_hbm, cell_ref), (shift_hbm, shift_ref), (weight_hbm, weight_ref), (x_hbm, x_ref),
        (gains_hbm, gains_ref), (basis_hbm, basis_ref),
    ]
    arrivals = [pltpu.make_async_copy(a, b, in_sem.at[n]) for n, (a, b) in enumerate(arrays)]
    departures = [pltpu.make_async_copy(out_ref.at[i], out_hbm.at[i], out_sem.at[i]) for i in range(N_IN)]
    departures.append(pltpu.make_async_copy(matrix_ref, matrix_hbm, out_sem.at[N_IN]))
    for copy in arrivals:
        copy.start()
    arrivals[0].wait()
    slot = slot_of_rows(owner_ref[...])
    spread(slot, place_ref)
    arrivals[1].wait()
    code = ((slot >> 3) & 1) * LANES + cell_ref[...] + 1
    lines = N_IN * 8
    held = jnp.where(iota((lines, ROWS), 0) == slot >> 4, code.astype(jnp.float32), 0.0).astype(jnp.bfloat16)
    lanes = jnp.where((iota((LANES, ROWS), 0) & 15) == (slot & 15), 1.0, 0.0).astype(jnp.bfloat16)
    codes = lax.dot_general(
        held, lanes, (((1,), (1,)), ((), ())), preferred_element_type=jnp.float32
    ).astype(jnp.bfloat16)
    for x in range(N_X):
        for i in range(N_IN):
            out_ref[i, x, CODES : CODES + 8, :] = codes[x // 2 * 8 : x // 2 * 8 + 8]
    for copy in arrivals[2:]:
        copy.wait()
    matrix_ref[...] = crossline_filter(gains_ref[...], basis_ref[...])
    departures[N_IN].start()
    chunk = iota((CHUNK, LANES), 1) >> 5

    def place(n):
        result = jnp.dot(
            place_ref[...], moved_ref[:, 3 * n * LANES : 3 * (n + 1) * LANES], preferred_element_type=jnp.float32
        )
        for g in range(N_IN):
            def part(quarter, unit):
                rows = slice(g * SLOTS + quarter * CHUNK, g * SLOTS + (quarter + 1) * CHUNK)
                a, b, c = (result[rows, k * LANES : (k + 1) * LANES] for k in range(3))
                if unit == 1:
                    return jnp.where(chunk == 3, a, b)
                if unit == 2:
                    return jnp.where(chunk == 0, c, b)
                return c if unit else a

            for unit in range(4):
                last = part(3, unit)
                for q in range(3):
                    out_ref[2 * n + unit // 2, 2 * g + unit % 2, q * CHUNK : (q + 1) * CHUNK, :] = jnp.where(
                        chunk == 3 - unit, pltpu.roll(last, CHUNK * (3 - q), 1), part(q, unit)
                    ).astype(jnp.bfloat16)
        departures[2 * n].start()
        departures[2 * n + 1].start()

    def all_tiles(narrow):
        refs = x_ref, shift_ref, weight_ref, places_ref, moved_ref

        if narrow:
            for n in range(TILES // 3 + 1):
                if n < TILES // 3:
                    for k in range(3 * n, 3 * n + 3):
                        for c in range(CLASSES):
                            moveout(
                                True, k, c,
                                lambda ref, c, at: jnp.broadcast_to(ref[c : c + 1, at], (8, LANES)),
                                slice(c * GROUP, (c + 1) * GROUP), *refs,
                            )
                if n:
                    place(n - 1)
            return

        def step(e, carry):
            tables = pl.ds(pl.multiple_of(e * 8, 8), 8)
            for c in range(8):
                rows = pl.ds(pl.multiple_of(e * 8 * GROUP + c * GROUP, GROUP), GROUP)
                for k in range(TILES):
                    moveout(
                        False, k, c,
                        lambda ref, c, at: jnp.broadcast_to(ref[tables, at][c : c + 1], (8, LANES)),
                        rows, *refs,
                    )
            return carry

        lax.fori_loop(0, CLASSES // 8, step, 0)
        for n in range(TILES // 3):
            place(n)

    narrow = table_places(shift_ref, places_ref)
    pl.when(narrow)(lambda: all_tiles(True))
    pl.when(jnp.logical_not(narrow))(lambda: all_tiles(False))
    for copy in departures:
        copy.wait()


def units():
    half = lax.axis_index("xline") & 1
    first = 2 * (lax.axis_index("inline") & 1)
    return half, first + half, first + 1 - half


def stack_kernel(slots_ref, keep_ref, send_ref, select_ref, stack_ref):
    half, unit, _ = units()
    bins = (iota((2 * LANES, LANES), 0) + 1).astype(jnp.float32).astype(jnp.bfloat16)
    depth = DEVICES * 16
    ones = jnp.ones((depth, LANES), jnp.bfloat16)
    lines = []
    for j in range(DEVICES // 8):
        line = jnp.zeros((8, LANES), jnp.float32)
        for g in range(8):
            mine = (iota((8, LANES), 1) >> 4) == g
            codes = slots_ref[8 * j + g, CODES : CODES + 8, :].astype(jnp.float32)
            line = jnp.where(mine, codes, line)
        lines.append(line)
    time = ((iota((2 * LANES, LANES), 1) >> 5) + unit) & 3

    def rows_of(first):
        return slots_ref[:, first : first + 16, :].reshape(depth, LANES)

    for p in range(8):
        for j in range(DEVICES // 8):
            row = jnp.broadcast_to(lines[j][p : p + 1], (16, LANES)).astype(jnp.bfloat16)
            row = jnp.concatenate([row] * 16, axis=0)
            select_ref[:, j * LANES : (j + 1) * LANES] = jnp.where(
                bins == row, jnp.bfloat16(1), jnp.bfloat16(0)
            )
        select = select_ref[...]

        def sums_of(a, b):
            both = jnp.dot(select, jnp.concatenate([a, b], axis=1), preferred_element_type=jnp.float32)
            return both[:, :LANES], both[:, LANES:]

        if p < 6:
            sums, fold = sums_of(rows_of(16 * p), ones)
        else:
            first, second = sums_of(rows_of(16 * (p - 6)), rows_of(CHUNK + 16 * (p - 6)))
            third, fold = sums_of(rows_of(2 * CHUNK + 16 * (p - 6)), ones)
            first, second, third = (
                pltpu.roll(part, CHUNK * (q + 1), 1) for q, part in enumerate((first, second, third))
            )
            sums = jnp.where(time == 0, first, jnp.where(time == 1, second, third))
        mean = (sums / jnp.maximum(fold, 1.0)).astype(jnp.bfloat16)
        stack_ref[2 * p] = mean[:LANES]
        stack_ref[2 * p + 1] = mean[LANES:]
    mine, other = pl.multiple_of(half * 64, 64), pl.multiple_of((1 - half) * 64, 64)
    send_ref[...] = stack_ref[:, pl.ds(other, 64), :]
    keep_ref[...] = stack_ref[:, pl.ds(mine, 64), :]


def filter_kernel(matrix_ref, keep_ref, received_ref, out_ref):
    half, own, neighbour = units()
    matrix = matrix_ref[...]
    for ref, start, unit in ((keep_ref, 96 * half, own), (received_ref, 96 * (1 - half), neighbour)):
        results = [
            lax.dot_general(
                ref[:, 16 * i : 16 * i + 16, :].reshape(N_X * 16, LANES),
                matrix,
                (((0,), (0,)), ((), ())),
                preferred_element_type=jnp.float32,
            )
            for i in range(4)
        ]
        for m in range(4):
            time = (m + unit) & 3

            @pl.when(time < 3)
            def _():
                for i in range(4):
                    out_ref[pl.ds(start + CHUNK * time, CHUNK), i, :] = results[i][m * CHUNK : (m + 1) * CHUNK]


def call(kernel, name, out_shape, scratch, in_specs, out_specs, mib):
    return pl.pallas_call(
        kernel,
        out_shape=out_shape,
        scratch_shapes=scratch,
        name=name,
        in_specs=in_specs,
        out_specs=out_specs,
        compiler_params=pltpu.CompilerParams(vmem_limit_bytes=mib * MIB),
    )


def exchange(block, axes):
    return lax.all_to_all(block, axes, split_axis=0, concat_axis=0, tiled=True)


def shards(traces, owner, cell, shift_table, weight_table, gains):
    bf16, dma = jnp.bfloat16, pltpu.SemaphoreType.DMA
    vmem = pl.BlockSpec(memory_space=pltpu.VMEM)
    hbm = pl.BlockSpec(memory_space=pltpu.HBM)
    owner_row, cell_row = owner.reshape(1, ROWS), cell.reshape(1, ROWS)
    out = (N_IN, N_X, CODES + 8, LANES)
    count = N_X * 16
    slots, matrix = call(
        pack_kernel,
        "pack",
        (jax.ShapeDtypeStruct(out, bf16), jax.ShapeDtypeStruct((count, count), bf16)),
        [
            pltpu.VMEM((1, ROWS), jnp.int32),
            pltpu.VMEM((1, ROWS), jnp.int32),
            pltpu.VMEM((1, count), jnp.float32),
            pltpu.VMEM((count, 2 * count), jnp.float32),
            pltpu.VMEM((CLASSES, SAMPLES), jnp.int32),
            pltpu.VMEM((CLASSES, SAMPLES), jnp.float32),
            pltpu.VMEM((ROWS, SAMPLES), bf16),
            pltpu.VMEM((count, count), bf16),
            pltpu.VMEM((4, CLASSES, SAMPLES), jnp.int32),
            pltpu.VMEM((ROWS, SAMPLES), bf16),
            pltpu.VMEM((N_IN * SLOTS, ROWS), bf16),
            pltpu.VMEM(out, bf16),
            dma((7,)),
            dma((N_IN + 1,)),
        ],
        [hbm] * 7,
        (hbm, hbm),
        60,
    )(owner_row, cell_row, gains.reshape(1, count), jnp.asarray(filter_basis()), shift_table, weight_table, traces)
    slots = exchange(slots.reshape(DEVICES, CODES + 8, LANES), ("inline", "xline"))
    part = jax.ShapeDtypeStruct((N_X, 64, LANES), bf16)
    keep, send = call(
        stack_kernel,
        "stack",
        (part, part),
        [pltpu.VMEM((2 * LANES, DEVICES * 16), bf16), pltpu.VMEM((N_X, LANES, LANES), bf16)],
        [vmem],
        (vmem, vmem),
        32,
    )(slots)
    received = lax.ppermute(send, "xline", [(x, x ^ 1) for x in range(N_X)])
    return call(
        filter_kernel,
        "crossline",
        jax.ShapeDtypeStruct((SAMPLES // N_IN, 4, N_X * 16), jnp.float32),
        [],
        [vmem] * 3,
        vmem,
        16,
    )(matrix, keep, received)


def solution(mesh):
    split = P(("inline", "xline"))
    placed = (P(("inline", "xline"), None), P(("inline", "xline"), None), split, P(), P(), P())
    return jax.shard_map(
        shards, mesh=mesh, in_specs=placed, out_specs=P("inline", "xline", None), check_vma=False
    )
```

```python
import functools

import numpy as np
import jax
import jax.numpy as jnp
from jax import lax
from jax.experimental import pallas as pl
from jax.experimental.pallas import tpu as pltpu
from jax.sharding import PartitionSpec as P

LANES = 128
ROWS = 512
SAMPLES = 1536
CLASSES = 32
GROUP = ROWS // CLASSES
TILES = SAMPLES // LANES
N_IN = 8
N_X = 16
DEVICES = N_IN * N_X
SLOTS = 128
CHUNK = 32
CODES = 96
MIB = 1024 * 1024


def iota(shape, dim):
    return lax.broadcasted_iota(jnp.int32, shape, dim)


def table_places(shift_ref, places_ref):
    lane = iota((8, LANES), 1)
    widest = jnp.zeros((8, 1), jnp.float32)
    for e in range(CLASSES // 8):
        rows = slice(8 * e, 8 * e + 8)
        for k in range(TILES):
            at = slice(k * LANES, (k + 1) * LANES)
            u = lane + shift_ref[rows, at]
            low = jnp.min(u.astype(jnp.float32), axis=1, keepdims=True)
            high = jnp.max(u.astype(jnp.float32), axis=1, keepdims=True)
            widest = jnp.maximum(widest, high - low)
            low = jnp.broadcast_to(low.astype(jnp.int32), (8, LANES))
            for step in range(2):
                places_ref[step, rows, at] = (u + step) & (LANES - 1)
                places_ref[2 + step, rows, at] = low + step + ((lane - low - step) & (LANES - 1))
    return jnp.max(widest) < LANES


def lanes_of(values, index):
    return jnp.take_along_axis(values, index, axis=1, mode="promise_in_bounds")


def first_below(u, sources):
    chosen = sources[2]
    for n in (1, 0):
        if sources[n] is not chosen:
            chosen = jnp.where(u < (n + 1) * LANES, sources[n], chosen)
    return chosen


def moveout(narrow, k, c, row_of, rows, x_ref, shift_ref, weight_ref, places_ref, moved_ref):
    at = slice(k * LANES, (k + 1) * LANES)
    weight = row_of(weight_ref, c, at)
    rest = 1.0 - weight
    blank = jnp.zeros((8, LANES), jnp.float32)
    halves = [[], []]
    for n in range(3):
        both = None
        if k + n < TILES:
            both = x_ref[rows, (k + n) * LANES : (k + n + 1) * LANES].astype(jnp.float32)
        halves[0].append(blank if both is None else both[:8])
        halves[1].append(blank if both is None else both[8:])
    parts = [[], []]
    for step in range(2):
        if narrow:
            index, held = row_of(places_ref.at[step], c, at), row_of(places_ref.at[2 + step], c, at)
            for h, sources in enumerate(halves):
                parts[h].append(lanes_of(first_below(held, sources), index))
        else:
            u = iota((8, LANES), 1) + row_of(shift_ref, c, at) + step
            for h, sources in enumerate(halves):
                got = [s if s is blank else lanes_of(s, u & (LANES - 1)) for s in sources]
                parts[h].append(first_below(u, got))
    mixed = [rest * first + weight * second for first, second in parts]
    moved_ref[rows, at] = jnp.concatenate(mixed, axis=0).astype(jnp.bfloat16)


def slot_of_rows(owner_row):
    owners = owner_row.astype(jnp.float32)
    blocks = [owners[:, b * LANES : (b + 1) * LANES] for b in range(ROWS // LANES)]
    columns = [jnp.transpose(jnp.broadcast_to(b, (LANES, LANES))) for b in blocks]
    earlier = iota((LANES, LANES), 0) < iota((LANES, LANES), 1)
    ranks = []
    for b, block in enumerate(blocks):
        total = jnp.zeros((LANES, LANES), jnp.float32)
        for a in range(b + 1):
            same = columns[a] == block
            if a == b:
                same = same & earlier
            total = total + jnp.where(same, 1.0, 0.0)
        ranks.append(jnp.sum(total, axis=0, keepdims=True))
    rank = jnp.concatenate(ranks, axis=1).astype(jnp.int32)
    return owner_row * 8 + rank


def spread(slot, place_ref):
    for m in range(N_IN * SLOTS // LANES):
        here = iota((LANES, ROWS), 0) + m * LANES == slot
        place_ref[m * LANES : (m + 1) * LANES, :] = jnp.where(here, 1.0, 0.0).astype(jnp.bfloat16)


def filter_basis():
    count = N_X * 16
    index = np.arange(count)
    phase = 2.0 * np.pi * (index[:, None] * index[None, :] % count) / count
    return np.concatenate([np.cos(phase), np.sin(phase)], axis=1).astype(np.float32)


def crossline_filter(gains, basis):
    count = basis.shape[0]
    scaled = basis * jnp.concatenate([gains, gains], axis=1)
    dims = (((1,), (1,)), ((), ()))
    product = lax.dot_general(
        scaled, basis, dims, precision=lax.Precision.HIGHEST, preferred_element_type=jnp.float32
    )
    return (product / count).astype(jnp.bfloat16)


def pack_kernel(
    owner_hbm, cell_hbm, gains_hbm, basis_hbm, shift_hbm, weight_hbm, x_hbm, out_hbm, matrix_hbm,
    owner_ref, cell_ref, gains_ref, basis_ref, shift_ref, weight_ref, x_ref, matrix_ref, places_ref, moved_ref, place_ref, out_ref, in_sem, out_sem,
):
    arrays = [
        (owner_hbm, owner_ref), (cell_hbm, cell_ref), (shift_hbm, shift_ref), (weight_hbm, weight_ref), (x_hbm, x_ref),
        (gains_hbm, gains_ref), (basis_hbm, basis_ref),
    ]
    arrivals = [pltpu.make_async_copy(a, b, in_sem.at[n]) for n, (a, b) in enumerate(arrays)]
    departures = [pltpu.make_async_copy(out_ref.at[i], out_hbm.at[i], out_sem.at[i]) for i in range(N_IN)]
    departures.append(pltpu.make_async_copy(matrix_ref, matrix_hbm, out_sem.at[N_IN]))
    for copy in arrivals:
        copy.start()
    arrivals[0].wait()
    slot = slot_of_rows(owner_ref[...])
    spread(slot, place_ref)
    arrivals[1].wait()
    code = ((slot >> 3) & 1) * LANES + cell_ref[...] + 1
    lines = N_IN * 8
    held = jnp.where(iota((lines, ROWS), 0) == slot >> 4, code.astype(jnp.float32), 0.0).astype(jnp.bfloat16)
    lanes = jnp.where((iota((LANES, ROWS), 0) & 15) == (slot & 15), 1.0, 0.0).astype(jnp.bfloat16)
    codes = lax.dot_general(
        held, lanes, (((1,), (1,)), ((), ())), preferred_element_type=jnp.float32
    ).astype(jnp.bfloat16)
    for x in range(N_X):
        for i in range(N_IN):
            out_ref[i, x, CODES : CODES + 8, :] = codes[x // 2 * 8 : x // 2 * 8 + 8]
    for copy in arrivals[2:]:
        copy.wait()
    matrix_ref[...] = crossline_filter(gains_ref[...], basis_ref[...])
    departures[N_IN].start()
    chunk = iota((CHUNK, LANES), 1) >> 5

    def place(n):
        result = jnp.dot(
            place_ref[...], moved_ref[:, 3 * n * LANES : 3 * (n + 1) * LANES], preferred_element_type=jnp.float32
        )
        for g in range(N_IN):
            def part(quarter, unit):
                rows = slice(g * SLOTS + quarter * CHUNK, g * SLOTS + (quarter + 1) * CHUNK)
                a, b, c = (result[rows, k * LANES : (k + 1) * LANES] for k in range(3))
                if unit == 1:
                    return jnp.where(chunk == 3, a, b)
                if unit == 2:
                    return jnp.where(chunk == 0, c, b)
                return c if unit else a

            for unit in range(4):
                last = part(3, unit)
                for q in range(3):
                    out_ref[2 * n + unit // 2, 2 * g + unit % 2, q * CHUNK : (q + 1) * CHUNK, :] = jnp.where(
                        chunk == 3 - unit, pltpu.roll(last, CHUNK * (3 - q), 1), part(q, unit)
                    ).astype(jnp.bfloat16)
        departures[2 * n].start()
        departures[2 * n + 1].start()

    def all_tiles(narrow):
        refs = x_ref, shift_ref, weight_ref, places_ref, moved_ref

        if narrow:
            for n in range(TILES // 3 + 1):
                if n < TILES // 3:
                    for k in range(3 * n, 3 * n + 3):
                        for c in range(CLASSES):
                            moveout(
                                True, k, c,
                                lambda ref, c, at: jnp.broadcast_to(ref[c : c + 1, at], (8, LANES)),
                                slice(c * GROUP, (c + 1) * GROUP), *refs,
                            )
                if n:
                    place(n - 1)
            return

        def step(e, carry):
            tables = pl.ds(pl.multiple_of(e * 8, 8), 8)
            for c in range(8):
                rows = pl.ds(pl.multiple_of(e * 8 * GROUP + c * GROUP, GROUP), GROUP)
                for k in range(TILES):
                    moveout(
                        False, k, c,
                        lambda ref, c, at: jnp.broadcast_to(ref[tables, at][c : c + 1], (8, LANES)),
                        rows, *refs,
                    )
            return carry

        lax.fori_loop(0, CLASSES // 8, step, 0)
        for n in range(TILES // 3):
            place(n)

    narrow = table_places(shift_ref, places_ref)
    pl.when(narrow)(lambda: all_tiles(True))
    pl.when(jnp.logical_not(narrow))(lambda: all_tiles(False))
    for copy in departures:
        copy.wait()


def units():
    half = lax.axis_index("xline") & 1
    first = 2 * (lax.axis_index("inline") & 1)
    return half, first + half, first + 1 - half


def stack_kernel(pairs, slots_ref, keep_ref, send_ref, select_ref, halves_ref):
    half, unit, _ = units()
    bins = (iota((2 * LANES, LANES), 0) + 1).astype(jnp.float32).astype(jnp.bfloat16)
    depth = DEVICES * 16
    ones = jnp.ones((depth, LANES), jnp.bfloat16)
    lines = []
    for j in range(DEVICES // 8):
        line = jnp.zeros((8, LANES), jnp.float32)
        for g in range(8):
            mine = (iota((8, LANES), 1) >> 4) == g
            codes = slots_ref[8 * j + g, CODES : CODES + 8, :].astype(jnp.float32)
            line = jnp.where(mine, codes, line)
        lines.append(line)
    time = ((iota((2 * LANES, LANES), 1) >> 5) + unit) & 3
    free = ((iota((16, LANES), 1) >> 5) + unit) & 3 == 3

    def rows_of(first):
        return slots_ref[:, first : first + 16, :].reshape(depth, LANES)

    for p in pairs:
        for j in range(DEVICES // 8):
            row = jnp.broadcast_to(lines[j][p : p + 1], (16, LANES)).astype(jnp.bfloat16)
            row = jnp.concatenate([row] * 16, axis=0)
            select_ref[:, j * LANES : (j + 1) * LANES] = jnp.where(
                bins == row, jnp.bfloat16(1), jnp.bfloat16(0)
            )
        select = select_ref[...]

        def sums_of(a, b):
            both = jnp.dot(select, jnp.concatenate([a, b], axis=1), preferred_element_type=jnp.float32)
            return both[:, :LANES], both[:, LANES:]

        if p < 6:
            sums, fold = sums_of(rows_of(16 * p), ones)
        else:
            first, second = sums_of(rows_of(16 * (p - 6)), rows_of(CHUNK + 16 * (p - 6)))
            third, fold = sums_of(rows_of(2 * CHUNK + 16 * (p - 6)), ones)
            first, second, third = (
                pltpu.roll(part, CHUNK * (q + 1), 1) for q, part in enumerate((first, second, third))
            )
            sums = jnp.where(time == 0, first, jnp.where(time == 1, second, third))
        mean = sums / jnp.maximum(fold, 1.0)
        for o in range(2):
            for h in range(2):
                four = [mean[o * LANES + h * 64 + 16 * i : o * LANES + h * 64 + 16 * i + 16] for i in range(4)]
                for i in range(3):
                    halves_ref[h, 2 * (p - pairs[0]) + o, 16 * i : 16 * i + 16, :] = jnp.where(
                        free, pltpu.roll(four[3], CHUNK * (3 - i), 1), four[i]
                    ).astype(jnp.bfloat16)
    send_ref[...] = halves_ref[1 - half]
    keep_ref[...] = halves_ref[half]


def filter_kernel(own, matrix_ref, first_ref, second_ref, *rest):
    out_hbm, slab_ref, sem = rest[-3:]
    half, own_unit, neighbour_unit = units()
    start, unit = (96 * half, own_unit) if own else (96 * (1 - half), neighbour_unit)
    matrix = matrix_ref[...]
    results = []
    for i in range(3):
        rows = [ref[:, 16 * i : 16 * i + 16, :].reshape(-1, LANES) for ref in (first_ref, second_ref)]
        results.append(
            lax.dot_general(
                jnp.concatenate(rows, axis=0),
                matrix,
                (((0,), (0,)), ((), ())),
                preferred_element_type=jnp.float32,
            )
        )
    for m in range(4):
        time = (m + unit) & 3
        parts = [result[m * CHUNK : (m + 1) * CHUNK] for result in results]

        @pl.when(time < 3)
        def _():
            for i in range(3):
                slab_ref[pl.ds(CHUNK * time, CHUNK), i, :] = parts[i]

        @pl.when(time == 3)
        def _():
            for i in range(3):
                slab_ref[CHUNK * i : CHUNK * (i + 1), 3, :] = parts[i]

    copy = pltpu.make_async_copy(slab_ref, out_hbm.at[pl.ds(start, 96)], sem)
    copy.start()
    copy.wait()


def call(kernel, name, out_shape, scratch, in_specs, out_specs, mib, aliases=None):
    return pl.pallas_call(
        kernel,
        out_shape=out_shape,
        scratch_shapes=scratch,
        name=name,
        in_specs=in_specs,
        out_specs=out_specs,
        input_output_aliases=aliases or {},
        compiler_params=pltpu.CompilerParams(vmem_limit_bytes=mib * MIB),
    )


def exchange(block, axes):
    return lax.all_to_all(block, axes, split_axis=0, concat_axis=0, tiled=True)


def shards(traces, owner, cell, shift_table, weight_table, gains):
    bf16, dma = jnp.bfloat16, pltpu.SemaphoreType.DMA
    vmem = pl.BlockSpec(memory_space=pltpu.VMEM)
    hbm = pl.BlockSpec(memory_space=pltpu.HBM)
    owner_row, cell_row = owner.reshape(1, ROWS), cell.reshape(1, ROWS)
    out = (N_IN, N_X, CODES + 8, LANES)
    count = N_X * 16
    slots, matrix = call(
        pack_kernel,
        "pack",
        (jax.ShapeDtypeStruct(out, bf16), jax.ShapeDtypeStruct((count, count), bf16)),
        [
            pltpu.VMEM((1, ROWS), jnp.int32),
            pltpu.VMEM((1, ROWS), jnp.int32),
            pltpu.VMEM((1, count), jnp.float32),
            pltpu.VMEM((count, 2 * count), jnp.float32),
            pltpu.VMEM((CLASSES, SAMPLES), jnp.int32),
            pltpu.VMEM((CLASSES, SAMPLES), jnp.float32),
            pltpu.VMEM((ROWS, SAMPLES), bf16),
            pltpu.VMEM((count, count), bf16),
            pltpu.VMEM((4, CLASSES, SAMPLES), jnp.int32),
            pltpu.VMEM((ROWS, SAMPLES), bf16),
            pltpu.VMEM((N_IN * SLOTS, ROWS), bf16),
            pltpu.VMEM(out, bf16),
            dma((7,)),
            dma((N_IN + 1,)),
        ],
        [hbm] * 7,
        (hbm, hbm),
        60,
    )(owner_row, cell_row, gains.reshape(1, count), jnp.asarray(filter_basis()), shift_table, weight_table, traces)
    slots = exchange(slots.reshape(DEVICES, CODES + 8, LANES), ("inline", "xline"))
    keep, received = [], []
    for pairs in (range(6), range(6, 8)):
        part = jax.ShapeDtypeStruct((2 * len(pairs), 48, LANES), bf16)
        kept, send = call(
            functools.partial(stack_kernel, pairs),
            f"stack_{pairs[0]}",
            (part, part),
            [pltpu.VMEM((2 * LANES, DEVICES * 16), bf16), pltpu.VMEM((2, *part.shape), bf16)],
            [vmem],
            (vmem, vmem),
            32,
        )(slots)
        keep.append(kept)
        received.append(lax.ppermute(send, "xline", [(x, x ^ 1) for x in range(N_X)]))
    result = jax.ShapeDtypeStruct((SAMPLES // N_IN, 4, count), jnp.float32)
    scratch = [pltpu.VMEM((96, 4, count), jnp.float32), dma]
    own = call(
        functools.partial(filter_kernel, True), "crossline_own", result, scratch, [vmem] * 3, hbm, 16
    )(matrix, *keep)
    return call(
        functools.partial(filter_kernel, False),
        "crossline_received",
        result,
        scratch,
        [vmem] * 3 + [hbm],
        hbm,
        16,
        {3: 0},
    )(matrix, *received, own)


def solution(mesh):
    split = P(("inline", "xline"))
    placed = (P(("inline", "xline"), None), P(("inline", "xline"), None), split, P(), P(), P())
    return jax.shard_map(
        shards, mesh=mesh, in_specs=placed, out_specs=P("inline", "xline", None), check_vma=False
    )
```

```python
import functools

import numpy as np
import jax
import jax.numpy as jnp
from jax import lax
from jax.experimental import pallas as pl
from jax.experimental.pallas import tpu as pltpu
from jax.sharding import PartitionSpec as P

LANES = 128
ROWS = 512
SAMPLES = 1536
CLASSES = 32
GROUP = ROWS // CLASSES
TILES = SAMPLES // LANES
N_IN = 8
N_X = 16
DEVICES = N_IN * N_X
SLOTS = 128
CHUNK = 32
BLOCK = (25, 4, LANES)
CODES = 24
MIB = 1024 * 1024


def iota(shape, dim):
    return lax.broadcasted_iota(jnp.int32, shape, dim)


def table_places(shift_ref, places_ref):
    lane = iota((8, LANES), 1)
    widest = jnp.zeros((8, 1), jnp.float32)
    for e in range(CLASSES // 8):
        rows = slice(8 * e, 8 * e + 8)
        for k in range(TILES):
            at = slice(k * LANES, (k + 1) * LANES)
            u = lane + shift_ref[rows, at]
            low = jnp.min(u.astype(jnp.float32), axis=1, keepdims=True)
            high = jnp.max(u.astype(jnp.float32), axis=1, keepdims=True)
            widest = jnp.maximum(widest, high - low)
            low = jnp.broadcast_to(low.astype(jnp.int32), (8, LANES))
            for step in range(2):
                places_ref[step, rows, at] = (u + step) & (LANES - 1)
                places_ref[2 + step, rows, at] = low + step + ((lane - low - step) & (LANES - 1))
    return jnp.max(widest) < LANES


def lanes_of(values, index):
    return jnp.take_along_axis(values, index, axis=1, mode="promise_in_bounds")


def first_below(u, sources):
    chosen = sources[2]
    for n in (1, 0):
        if sources[n] is not chosen:
            chosen = jnp.where(u < (n + 1) * LANES, sources[n], chosen)
    return chosen


def moveout(narrow, k, c, row_of, rows, x_ref, shift_ref, weight_ref, places_ref, moved_ref):
    at = slice(k * LANES, (k + 1) * LANES)
    weight = row_of(weight_ref, c, at)
    rest = 1.0 - weight
    blank = jnp.zeros((8, LANES), jnp.float32)
    halves = [[], []]
    for n in range(3):
        both = None
        if k + n < TILES:
            both = x_ref[rows, (k + n) * LANES : (k + n + 1) * LANES].astype(jnp.float32)
        halves[0].append(blank if both is None else both[:8])
        halves[1].append(blank if both is None else both[8:])
    parts = [[], []]
    for step in range(2):
        if narrow:
            index, held = row_of(places_ref.at[step], c, at), row_of(places_ref.at[2 + step], c, at)
            for h, sources in enumerate(halves):
                parts[h].append(lanes_of(first_below(held, sources), index))
        else:
            u = iota((8, LANES), 1) + row_of(shift_ref, c, at) + step
            for h, sources in enumerate(halves):
                got = [s if s is blank else lanes_of(s, u & (LANES - 1)) for s in sources]
                parts[h].append(first_below(u, got))
    mixed = [rest * first + weight * second for first, second in parts]
    moved_ref[rows, at] = jnp.concatenate(mixed, axis=0).astype(jnp.bfloat16)


def slot_of_rows(owner_row):
    owners = owner_row.astype(jnp.float32)
    blocks = [owners[:, b * LANES : (b + 1) * LANES] for b in range(ROWS // LANES)]
    columns = [jnp.transpose(jnp.broadcast_to(b, (LANES, LANES))) for b in blocks]
    earlier = iota((LANES, LANES), 0) < iota((LANES, LANES), 1)
    ranks = []
    for b, block in enumerate(blocks):
        total = jnp.zeros((LANES, LANES), jnp.float32)
        for a in range(b + 1):
            same = columns[a] == block
            if a == b:
                same = same & earlier
            total = total + jnp.where(same, 1.0, 0.0)
        ranks.append(jnp.sum(total, axis=0, keepdims=True))
    rank = jnp.concatenate(ranks, axis=1).astype(jnp.int32)
    return owner_row * 8 + rank


def spread(slot, place_ref):
    for m in range(N_IN * SLOTS // LANES):
        here = iota((LANES, ROWS), 0) + m * LANES == slot
        place_ref[m * LANES : (m + 1) * LANES, :] = jnp.where(here, 1.0, 0.0).astype(jnp.bfloat16)


def filter_basis():
    count = N_X * 16
    index = np.arange(count)
    phase = 2.0 * np.pi * (index[:, None] * index[None, :] % count) / count
    return np.concatenate([np.cos(phase), np.sin(phase)], axis=1).astype(np.float32)


def matrix_kernel(gains_ref, basis_ref, matrix_ref):
    gains, basis = gains_ref[...], basis_ref[...]
    scaled = basis * jnp.concatenate([gains, gains], axis=1)
    dims = (((1,), (1,)), ((), ()))
    product = lax.dot_general(
        scaled, basis, dims, precision=lax.Precision.HIGHEST, preferred_element_type=jnp.float32
    )
    matrix_ref[...] = (product / basis.shape[0]).astype(jnp.bfloat16)


def pack_kernel(
    owner_hbm, cell_hbm, shift_hbm, weight_hbm, x_hbm, out_hbm,
    owner_ref, cell_ref, shift_ref, weight_ref, x_ref, places_ref, moved_ref, place_ref, out_ref, in_sem, out_sem,
):
    arrays = [
        (owner_hbm, owner_ref), (cell_hbm, cell_ref), (shift_hbm, shift_ref), (weight_hbm, weight_ref), (x_hbm, x_ref),
    ]
    arrivals = [pltpu.make_async_copy(a, b, in_sem.at[n]) for n, (a, b) in enumerate(arrays)]
    departures = [pltpu.make_async_copy(out_ref.at[i], out_hbm.at[i], out_sem.at[i]) for i in range(N_IN)]
    for copy in arrivals:
        copy.start()
    arrivals[0].wait()
    slot = slot_of_rows(owner_ref[...])
    spread(slot, place_ref)
    arrivals[1].wait()
    code = ((slot >> 3) & 1) * LANES + cell_ref[...] + 1
    lines = N_IN * 4
    held = jnp.where(iota((lines, ROWS), 0) == slot >> 5, code.astype(jnp.float32), 0.0).astype(jnp.bfloat16)
    lanes = jnp.where((iota((LANES, ROWS), 0) & 31) == (slot & 31), 1.0, 0.0).astype(jnp.bfloat16)
    codes = lax.dot_general(
        held, lanes, (((1,), (1,)), ((), ())), preferred_element_type=jnp.float32
    ).astype(jnp.bfloat16).reshape(N_IN, 4, LANES)
    for x in range(N_X):
        for i in range(N_IN):
            out_ref[i, x, CODES] = codes[x // 2]
    for copy in arrivals[2:]:
        copy.wait()
    chunk = iota((CHUNK, LANES), 1) >> 5

    def place(n):
        result = jnp.dot(
            place_ref[...], moved_ref[:, 3 * n * LANES : 3 * (n + 1) * LANES], preferred_element_type=jnp.float32
        )
        for g in range(N_IN):
            def part(quarter, unit):
                rows = slice(g * SLOTS + quarter * CHUNK, g * SLOTS + (quarter + 1) * CHUNK)
                a, b, c = (result[rows, k * LANES : (k + 1) * LANES] for k in range(3))
                if unit == 1:
                    return jnp.where(chunk == 3, a, b)
                if unit == 2:
                    return jnp.where(chunk == 0, c, b)
                return c if unit else a

            for unit in range(4):
                last = part(3, unit)
                for q in range(3):
                    block = jnp.where(chunk == 3 - unit, pltpu.roll(last, CHUNK * (3 - q), 1), part(q, unit))
                    out_ref[2 * n + unit // 2, 2 * g + unit % 2, 8 * q : 8 * q + 8] = block.astype(
                        jnp.bfloat16
                    ).reshape(8, 4, LANES)
        departures[2 * n].start()
        departures[2 * n + 1].start()

    def all_tiles(narrow):
        refs = x_ref, shift_ref, weight_ref, places_ref, moved_ref

        if narrow:
            for n in range(TILES // 3 + 1):
                if n < TILES // 3:
                    for k in range(3 * n, 3 * n + 3):
                        for c in range(CLASSES):
                            moveout(
                                True, k, c,
                                lambda ref, c, at: jnp.broadcast_to(ref[c : c + 1, at], (8, LANES)),
                                slice(c * GROUP, (c + 1) * GROUP), *refs,
                            )
                if n:
                    place(n - 1)
            return

        def step(e, carry):
            tables = pl.ds(pl.multiple_of(e * 8, 8), 8)
            for c in range(8):
                rows = pl.ds(pl.multiple_of(e * 8 * GROUP + c * GROUP, GROUP), GROUP)
                for k in range(TILES):
                    moveout(
                        False, k, c,
                        lambda ref, c, at: jnp.broadcast_to(ref[tables, at][c : c + 1], (8, LANES)),
                        rows, *refs,
                    )
            return carry

        lax.fori_loop(0, CLASSES // 8, step, 0)
        for n in range(TILES // 3):
            place(n)

    narrow = table_places(shift_ref, places_ref)
    pl.when(narrow)(lambda: all_tiles(True))
    pl.when(jnp.logical_not(narrow))(lambda: all_tiles(False))
    for copy in departures:
        copy.wait()


def units():
    half = lax.axis_index("xline") & 1
    first = 2 * (lax.axis_index("inline") & 1)
    return half, first + half, first + 1 - half


def stack_kernel(pairs, slots_ref, keep_ref, send_ref, select_ref, halves_ref):
    half, unit, _ = units()
    bins = (iota((2 * LANES, LANES), 0) + 1).astype(jnp.float32).astype(jnp.bfloat16)
    depth = DEVICES * 16
    ones = jnp.ones((depth, LANES), jnp.bfloat16)
    group = iota((4, LANES), 1) >> 4
    lines = []
    for j in range(DEVICES // 8):
        here = there = jnp.zeros((4, LANES), jnp.float32)
        for g in range(8):
            codes = slots_ref[8 * j + g, CODES].astype(jnp.float32)
            here = jnp.where(group == g, codes, here)
            there = jnp.where(group == (g - 1) % 8, codes, there)
        there = pltpu.roll(there, 16, 1)
        lines.append([jnp.where(group & 1 == parity, here, there) for parity in range(2)])
    time = ((iota((2 * LANES, LANES), 1) >> 5) + unit) & 3
    free = ((iota((16, LANES), 1) >> 5) + unit) & 3 == 3

    def rows_of(first):
        return slots_ref[:, first // 4 : first // 4 + 4].reshape(depth, LANES)

    for p in pairs:
        for j in range(DEVICES // 8):
            row = jnp.broadcast_to(lines[j][p & 1][p >> 1 : (p >> 1) + 1], (16, LANES)).astype(jnp.bfloat16)
            row = jnp.concatenate([row] * 16, axis=0)
            select_ref[:, j * LANES : (j + 1) * LANES] = jnp.where(
                bins == row, jnp.bfloat16(1), jnp.bfloat16(0)
            )
        select = select_ref[...]

        def sums_of(a, b):
            both = jnp.dot(select, jnp.concatenate([a, b], axis=1), preferred_element_type=jnp.float32)
            return both[:, :LANES], both[:, LANES:]

        if p < 6:
            sums, fold = sums_of(rows_of(16 * p), ones)
        else:
            first, second = sums_of(rows_of(16 * (p - 6)), rows_of(CHUNK + 16 * (p - 6)))
            third, fold = sums_of(rows_of(2 * CHUNK + 16 * (p - 6)), ones)
            first, second, third = (
                pltpu.roll(part, CHUNK * (q + 1), 1) for q, part in enumerate((first, second, third))
            )
            sums = jnp.where(time == 0, first, jnp.where(time == 1, second, third))
        mean = sums / jnp.maximum(fold, 1.0)
        for o in range(2):
            for h in range(2):
                four = [mean[o * LANES + h * 64 + 16 * i : o * LANES + h * 64 + 16 * i + 16] for i in range(4)]
                for i in range(3):
                    halves_ref[h, 2 * (p - pairs[0]) + o, 16 * i : 16 * i + 16, :] = jnp.where(
                        free, pltpu.roll(four[3], CHUNK * (3 - i), 1), four[i]
                    ).astype(jnp.bfloat16)
    send_ref[...] = halves_ref[1 - half]
    keep_ref[...] = halves_ref[half]


def filter_kernel(own, matrix_ref, first_ref, second_ref, *rest):
    out_hbm, slab_ref, sem = rest[-3:]
    half, own_unit, neighbour_unit = units()
    start, unit = (96 * half, own_unit) if own else (96 * (1 - half), neighbour_unit)
    matrix = matrix_ref[...]
    results = []
    for i in range(3):
        rows = [ref[:, 16 * i : 16 * i + 16, :].reshape(-1, LANES) for ref in (first_ref, second_ref)]
        results.append(
            lax.dot_general(
                jnp.concatenate(rows, axis=0),
                matrix,
                (((0,), (0,)), ((), ())),
                preferred_element_type=jnp.float32,
            )
        )
    for m in range(4):
        time = (m + unit) & 3
        parts = [result[m * CHUNK : (m + 1) * CHUNK] for result in results]

        @pl.when(time < 3)
        def _():
            for i in range(3):
                slab_ref[pl.ds(CHUNK * time, CHUNK), i, :] = parts[i]

        @pl.when(time == 3)
        def _():
            for i in range(3):
                slab_ref[CHUNK * i : CHUNK * (i + 1), 3, :] = parts[i]

    copy = pltpu.make_async_copy(slab_ref, out_hbm.at[pl.ds(start, 96)], sem)
    copy.start()
    copy.wait()


def call(kernel, name, out_shape, scratch, in_specs, out_specs, mib, aliases=None):
    return pl.pallas_call(
        kernel,
        out_shape=out_shape,
        scratch_shapes=scratch,
        name=name,
        in_specs=in_specs,
        out_specs=out_specs,
        input_output_aliases=aliases or {},
        compiler_params=pltpu.CompilerParams(vmem_limit_bytes=mib * MIB),
    )


def exchange(block, axes):
    return lax.all_to_all(block, axes, split_axis=0, concat_axis=0, tiled=True)


def shards(traces, owner, cell, shift_table, weight_table, gains):
    bf16, dma = jnp.bfloat16, pltpu.SemaphoreType.DMA
    vmem = pl.BlockSpec(memory_space=pltpu.VMEM)
    hbm = pl.BlockSpec(memory_space=pltpu.HBM)
    owner_row, cell_row = owner.reshape(1, ROWS), cell.reshape(1, ROWS)
    out = (N_IN, N_X, *BLOCK)
    count = N_X * 16
    slots = call(
        pack_kernel,
        "pack",
        jax.ShapeDtypeStruct(out, bf16),
        [
            pltpu.VMEM((1, ROWS), jnp.int32),
            pltpu.VMEM((1, ROWS), jnp.int32),
            pltpu.VMEM((CLASSES, SAMPLES), jnp.int32),
            pltpu.VMEM((CLASSES, SAMPLES), jnp.float32),
            pltpu.VMEM((ROWS, SAMPLES), bf16),
            pltpu.VMEM((4, CLASSES, SAMPLES), jnp.int32),
            pltpu.VMEM((ROWS, SAMPLES), bf16),
            pltpu.VMEM((N_IN * SLOTS, ROWS), bf16),
            pltpu.VMEM(out, bf16),
            dma((5,)),
            dma((N_IN,)),
        ],
        [hbm] * 5,
        hbm,
        60,
    )(owner_row, cell_row, shift_table, weight_table, traces)
    matrix = call(
        matrix_kernel, "matrix", jax.ShapeDtypeStruct((count, count), bf16), [], [vmem] * 2, vmem, 16
    )(gains.reshape(1, count), jnp.asarray(filter_basis()))
    slots = exchange(slots.reshape(DEVICES, *BLOCK), ("inline", "xline"))
    slots, matrix = lax.optimization_barrier((slots, matrix))
    keep, received = [], []
    for pairs in (range(6), range(6, 8)):
        part = jax.ShapeDtypeStruct((2 * len(pairs), 48, LANES), bf16)
        kept, send = call(
            functools.partial(stack_kernel, pairs),
            f"stack_{pairs[0]}",
            (part, part),
            [pltpu.VMEM((2 * LANES, DEVICES * 16), bf16), pltpu.VMEM((2, *part.shape), bf16)],
            [vmem],
            (vmem, vmem),
            32,
        )(slots)
        keep.append(kept)
        received.append(lax.ppermute(send, "xline", [(x, x ^ 1) for x in range(N_X)]))
    result = jax.ShapeDtypeStruct((SAMPLES // N_IN, 4, count), jnp.float32)
    scratch = [pltpu.VMEM((96, 4, count), jnp.float32), dma]
    own = call(
        functools.partial(filter_kernel, True), "crossline_own", result, scratch, [vmem] * 3, hbm, 16
    )(matrix, *keep)
    return call(
        functools.partial(filter_kernel, False),
        "crossline_received",
        result,
        scratch,
        [vmem] * 3 + [hbm],
        hbm,
        16,
        {3: 0},
    )(matrix, *received, own)


def solution(mesh):
    split = P(("inline", "xline"))
    placed = (P(("inline", "xline"), None), P(("inline", "xline"), None), split, P(), P(), P())
    return jax.shard_map(
        shards, mesh=mesh, in_specs=placed, out_specs=P("inline", "xline", None), check_vma=False
    )
```

```python
import functools

import numpy as np
import jax
import jax.numpy as jnp
from jax import lax
from jax.experimental import pallas as pl
from jax.experimental.pallas import tpu as pltpu
from jax.sharding import PartitionSpec as P

LANES = 128
ROWS = 512
SAMPLES = 1536
CLASSES = 32
GROUP = ROWS // CLASSES
TILES = SAMPLES // LANES
N_IN = 8
N_X = 16
DEVICES = N_IN * N_X
SLOTS = 128
CHUNK = 32
BLOCK = (25, 4, LANES)
CODES = 24
MIB = 1024 * 1024


def iota(shape, dim):
    return lax.broadcasted_iota(jnp.int32, shape, dim)


def table_places(shift_ref, places_ref):
    lane = iota((8, LANES), 1)
    widest = jnp.zeros((8, 1), jnp.float32)
    for e in range(CLASSES // 8):
        rows = slice(8 * e, 8 * e + 8)
        for k in range(TILES):
            at = slice(k * LANES, (k + 1) * LANES)
            u = lane + shift_ref[rows, at]
            low = jnp.min(u.astype(jnp.float32), axis=1, keepdims=True)
            high = jnp.max(u.astype(jnp.float32), axis=1, keepdims=True)
            widest = jnp.maximum(widest, high - low)
            low = jnp.broadcast_to(low.astype(jnp.int32), (8, LANES))
            for step in range(2):
                places_ref[step, rows, at] = (u + step) & (LANES - 1)
                places_ref[2 + step, rows, at] = low + step + ((lane - low - step) & (LANES - 1))
    return jnp.max(widest) < LANES


def lanes_of(values, index):
    return jnp.take_along_axis(values, index, axis=1, mode="promise_in_bounds")


def first_below(u, sources):
    chosen = sources[2]
    for n in (1, 0):
        if sources[n] is not chosen:
            chosen = jnp.where(u < (n + 1) * LANES, sources[n], chosen)
    return chosen


def moveout(narrow, k, c, row_of, rows, x_ref, shift_ref, weight_ref, places_ref, moved_ref):
    at = slice(k * LANES, (k + 1) * LANES)
    weight = row_of(weight_ref, c, at)
    rest = 1.0 - weight
    blank = jnp.zeros((8, LANES), jnp.float32)
    halves = [[], []]
    for n in range(3):
        both = None
        if k + n < TILES:
            both = x_ref[rows, (k + n) * LANES : (k + n + 1) * LANES].astype(jnp.float32)
        halves[0].append(blank if both is None else both[:8])
        halves[1].append(blank if both is None else both[8:])
    parts = [[], []]
    for step in range(2):
        if narrow:
            index, held = row_of(places_ref.at[step], c, at), row_of(places_ref.at[2 + step], c, at)
            for h, sources in enumerate(halves):
                parts[h].append(lanes_of(first_below(held, sources), index))
        else:
            u = iota((8, LANES), 1) + row_of(shift_ref, c, at) + step
            for h, sources in enumerate(halves):
                got = [s if s is blank else lanes_of(s, u & (LANES - 1)) for s in sources]
                parts[h].append(first_below(u, got))
    mixed = [rest * first + weight * second for first, second in parts]
    moved_ref[rows, at] = jnp.concatenate(mixed, axis=0).astype(jnp.bfloat16)


def slot_of_rows(owner_row):
    owners = owner_row.astype(jnp.float32)
    blocks = [owners[:, b * LANES : (b + 1) * LANES] for b in range(ROWS // LANES)]
    columns = [jnp.transpose(jnp.broadcast_to(b, (LANES, LANES))) for b in blocks]
    earlier = iota((LANES, LANES), 0) < iota((LANES, LANES), 1)
    ranks = []
    for b, block in enumerate(blocks):
        total = jnp.zeros((LANES, LANES), jnp.float32)
        for a in range(b + 1):
            same = columns[a] == block
            if a == b:
                same = same & earlier
            total = total + jnp.where(same, 1.0, 0.0)
        ranks.append(jnp.sum(total, axis=0, keepdims=True))
    rank = jnp.concatenate(ranks, axis=1).astype(jnp.int32)
    return owner_row * 8 + rank


def spread(slot, place_ref):
    for m in range(N_IN * SLOTS // LANES):
        here = iota((LANES, ROWS), 0) + m * LANES == slot
        place_ref[m * LANES : (m + 1) * LANES, :] = jnp.where(here, 1.0, 0.0).astype(jnp.bfloat16)


def filter_basis():
    count = N_X * 16
    index = np.arange(count)
    phase = 2.0 * np.pi * (index[:, None] * index[None, :] % count) / count
    return np.concatenate([np.cos(phase), np.sin(phase)], axis=1).astype(np.float32)


def matrix_kernel(gains_ref, basis_ref, matrix_ref):
    gains, basis = gains_ref[...], basis_ref[...]
    scaled = basis * jnp.concatenate([gains, gains], axis=1)
    dims = (((1,), (1,)), ((), ()))
    product = lax.dot_general(
        scaled, basis, dims, precision=lax.Precision.HIGHEST, preferred_element_type=jnp.float32
    )
    matrix_ref[...] = (product / basis.shape[0]).astype(jnp.bfloat16)


def pack_kernel(
    owner_hbm, cell_hbm, shift_hbm, weight_hbm, x_hbm, out_hbm,
    owner_ref, cell_ref, shift_ref, weight_ref, x_ref, places_ref, moved_ref, place_ref, out_ref, in_sem, out_sem,
):
    arrays = [
        (owner_hbm, owner_ref), (cell_hbm, cell_ref), (shift_hbm, shift_ref), (weight_hbm, weight_ref), (x_hbm, x_ref),
    ]
    arrivals = [pltpu.make_async_copy(a, b, in_sem.at[n]) for n, (a, b) in enumerate(arrays)]
    departures = [pltpu.make_async_copy(out_ref.at[i], out_hbm.at[i], out_sem.at[i]) for i in range(N_IN)]
    for copy in arrivals:
        copy.start()
    arrivals[0].wait()
    slot = slot_of_rows(owner_ref[...])
    spread(slot, place_ref)
    arrivals[1].wait()
    code = cell_ref[...] + 1
    lines = N_IN * 4
    held = jnp.where(iota((lines, ROWS), 0) == slot >> 5, code.astype(jnp.float32), 0.0).astype(jnp.bfloat16)
    lanes = jnp.where((iota((LANES, ROWS), 0) & 31) == (slot & 31), 1.0, 0.0).astype(jnp.bfloat16)
    codes = lax.dot_general(
        held, lanes, (((1,), (1,)), ((), ())), preferred_element_type=jnp.float32
    ).astype(jnp.bfloat16).reshape(N_IN, 4, LANES)
    for x in range(N_X):
        for i in range(N_IN):
            out_ref[i, x, CODES] = codes[x // 2]
    arrivals[2].wait()
    narrow = table_places(shift_ref, places_ref)
    arrivals[3].wait()
    arrivals[4].wait()
    chunk = iota((CHUNK, LANES), 1) >> 5

    def place(n):
        result = jnp.dot(
            place_ref[...], moved_ref[:, 3 * n * LANES : 3 * (n + 1) * LANES], preferred_element_type=jnp.float32
        )
        for g in range(N_IN):
            def part(quarter, unit):
                rows = slice(g * SLOTS + quarter * CHUNK, g * SLOTS + (quarter + 1) * CHUNK)
                a, b, c = (result[rows, k * LANES : (k + 1) * LANES] for k in range(3))
                if unit == 1:
                    return jnp.where(chunk == 3, a, b)
                if unit == 2:
                    return jnp.where(chunk == 0, c, b)
                return c if unit else a

            for unit in range(4):
                last = part(3, unit)
                for q in range(3):
                    block = jnp.where(chunk == 3 - unit, pltpu.roll(last, CHUNK * (3 - q), 1), part(q, unit))
                    out_ref[2 * n + unit // 2, 2 * g + unit % 2, 8 * q : 8 * q + 8] = block.astype(
                        jnp.bfloat16
                    ).reshape(8, 4, LANES)
        departures[2 * n].start()
        departures[2 * n + 1].start()

    def all_tiles(narrow):
        refs = x_ref, shift_ref, weight_ref, places_ref, moved_ref

        if narrow:
            for n in range(TILES // 3 + 1):
                if n < TILES // 3:
                    for k in range(3 * n, 3 * n + 3):
                        for c in range(CLASSES):
                            moveout(
                                True, k, c,
                                lambda ref, c, at: jnp.broadcast_to(ref[c : c + 1, at], (8, LANES)),
                                slice(c * GROUP, (c + 1) * GROUP), *refs,
                            )
                if n:
                    place(n - 1)
            return

        def step(e, carry):
            tables = pl.ds(pl.multiple_of(e * 8, 8), 8)
            for c in range(8):
                rows = pl.ds(pl.multiple_of(e * 8 * GROUP + c * GROUP, GROUP), GROUP)
                for k in range(TILES):
                    moveout(
                        False, k, c,
                        lambda ref, c, at: jnp.broadcast_to(ref[tables, at][c : c + 1], (8, LANES)),
                        rows, *refs,
                    )
            return carry

        lax.fori_loop(0, CLASSES // 8, step, 0)
        for n in range(TILES // 3):
            place(n)

    pl.when(narrow)(lambda: all_tiles(True))
    pl.when(jnp.logical_not(narrow))(lambda: all_tiles(False))
    for copy in departures:
        copy.wait()


def units():
    half = lax.axis_index("xline") & 1
    first = 2 * (lax.axis_index("inline") & 1)
    return half, first + half, first + 1 - half


def stack_kernel(owners, slots_ref, keep_ref, send_ref, select_ref, halves_ref):
    half, unit, _ = units()
    bins = (iota((LANES, LANES), 0) + 1).astype(jnp.float32).astype(jnp.bfloat16)
    depth = DEVICES * 8
    ones = jnp.ones((depth, LANES), jnp.bfloat16)
    group = iota((4, LANES), 1) >> 3
    at = [group == g for g in range(16)]
    apart = [[((group - c) & 3) == d for d in range(4)] for c in range(4)]
    lines = []
    for j in range(DEVICES // 16):
        turned = [jnp.zeros((4, LANES), jnp.float32) for _ in range(4)]
        for g in range(16):
            codes = slots_ref[16 * j + g, CODES].astype(jnp.float32)
            turned = [jnp.where(at[(g - d) % 16], codes, turned[d]) for d in range(4)]
        turned = [turned[0]] + [pltpu.roll(turned[d], 8 * d, 1) for d in range(1, 4)]
        lines.append([])
        for c in range(4):
            line = turned[0]
            for d in range(1, 4):
                line = jnp.where(apart[c][d], turned[d], line)
            lines[j].append(line)
    time = ((iota((LANES, LANES), 1) >> 5) + unit) & 3
    free = ((iota((16, LANES), 1) >> 5) + unit) & 3 == 3

    def rows_of(first):
        return slots_ref[:, first // 4 : first // 4 + 2].reshape(depth, LANES)

    for o in owners:
        for j in range(DEVICES // 16):
            row = jnp.broadcast_to(lines[j][o % 4][o // 4 : o // 4 + 1], (16, LANES)).astype(jnp.bfloat16)
            row = jnp.concatenate([row] * 8, axis=0)
            select_ref[:, j * LANES : (j + 1) * LANES] = jnp.where(
                bins == row, jnp.bfloat16(1), jnp.bfloat16(0)
            )
        select = select_ref[...]

        def sums_of(a, b):
            both = jnp.dot(select, jnp.concatenate([a, b], axis=1), preferred_element_type=jnp.float32)
            return both[:, :LANES], both[:, LANES:]

        if o < 12:
            sums, fold = sums_of(rows_of(8 * o), ones)
        else:
            first, second = sums_of(rows_of(8 * (o - 12)), rows_of(CHUNK + 8 * (o - 12)))
            third, fold = sums_of(rows_of(2 * CHUNK + 8 * (o - 12)), ones)
            first, second, third = (
                pltpu.roll(part, CHUNK * (q + 1), 1) for q, part in enumerate((first, second, third))
            )
            sums = jnp.where(time == 0, first, jnp.where(time == 1, second, third))
        mean = sums / jnp.maximum(fold, 1.0)
        for h in range(2):
            four = [mean[h * 64 + 16 * i : h * 64 + 16 * i + 16] for i in range(4)]
            for i in range(3):
                halves_ref[h, o - owners[0], 16 * i : 16 * i + 16, :] = jnp.where(
                    free, pltpu.roll(four[3], CHUNK * (3 - i), 1), four[i]
                ).astype(jnp.bfloat16)
    send_ref[...] = halves_ref[1 - half]
    keep_ref[...] = halves_ref[half]


def filter_kernel(own, matrix_ref, first_ref, second_ref, *rest):
    out_hbm, slab_ref, sem = rest[-3:]
    half, own_unit, neighbour_unit = units()
    start, unit = (96 * half, own_unit) if own else (96 * (1 - half), neighbour_unit)
    matrix = matrix_ref[...]
    results = []
    for i in range(3):
        rows = [ref[:, 16 * i : 16 * i + 16, :].reshape(-1, LANES) for ref in (first_ref, second_ref)]
        results.append(
            lax.dot_general(
                jnp.concatenate(rows, axis=0),
                matrix,
                (((0,), (0,)), ((), ())),
                preferred_element_type=jnp.float32,
            )
        )
    for m in range(4):
        time = (m + unit) & 3
        parts = [result[m * CHUNK : (m + 1) * CHUNK] for result in results]

        @pl.when(time < 3)
        def _():
            for i in range(3):
                slab_ref[pl.ds(CHUNK * time, CHUNK), i, :] = parts[i]

        @pl.when(time == 3)
        def _():
            for i in range(3):
                slab_ref[CHUNK * i : CHUNK * (i + 1), 3, :] = parts[i]

    copy = pltpu.make_async_copy(slab_ref, out_hbm.at[pl.ds(start, 96)], sem)
    copy.start()
    copy.wait()


def call(kernel, name, out_shape, scratch, in_specs, out_specs, mib, aliases=None):
    return pl.pallas_call(
        kernel,
        out_shape=out_shape,
        scratch_shapes=scratch,
        name=name,
        in_specs=in_specs,
        out_specs=out_specs,
        input_output_aliases=aliases or {},
        compiler_params=pltpu.CompilerParams(vmem_limit_bytes=mib * MIB),
    )


def exchange(block, axes):
    return lax.all_to_all(block, axes, split_axis=0, concat_axis=0, tiled=True)


def shards(traces, owner, cell, shift_table, weight_table, gains):
    bf16, dma = jnp.bfloat16, pltpu.SemaphoreType.DMA
    vmem = pl.BlockSpec(memory_space=pltpu.VMEM)
    hbm = pl.BlockSpec(memory_space=pltpu.HBM)
    owner_row, cell_row = owner.reshape(1, ROWS), cell.reshape(1, ROWS)
    out = (N_IN, N_X, *BLOCK)
    count = N_X * 16
    slots = call(
        pack_kernel,
        "pack",
        jax.ShapeDtypeStruct(out, bf16),
        [
            pltpu.VMEM((1, ROWS), jnp.int32),
            pltpu.VMEM((1, ROWS), jnp.int32),
            pltpu.VMEM((CLASSES, SAMPLES), jnp.int32),
            pltpu.VMEM((CLASSES, SAMPLES), jnp.float32),
            pltpu.VMEM((ROWS, SAMPLES), bf16),
            pltpu.VMEM((4, CLASSES, SAMPLES), jnp.int32),
            pltpu.VMEM((ROWS, SAMPLES), bf16),
            pltpu.VMEM((N_IN * SLOTS, ROWS), bf16),
            pltpu.VMEM(out, bf16),
            dma((5,)),
            dma((N_IN,)),
        ],
        [hbm] * 5,
        hbm,
        60,
    )(owner_row, cell_row, shift_table, weight_table, traces)
    matrix = call(
        matrix_kernel, "matrix", jax.ShapeDtypeStruct((count, count), bf16), [], [vmem] * 2, vmem, 16
    )(gains.reshape(1, count), jnp.asarray(filter_basis()))
    slots = exchange(slots.reshape(DEVICES, *BLOCK), ("inline", "xline"))
    slots, matrix = lax.optimization_barrier((slots, matrix))
    keep, received = [], []
    for owners in (range(12), range(12, 16)):
        part = jax.ShapeDtypeStruct((len(owners), 48, LANES), bf16)
        kept, send = call(
            functools.partial(stack_kernel, owners),
            f"stack_{owners[0]}",
            (part, part),
            [pltpu.VMEM((LANES, DEVICES * 8), bf16), pltpu.VMEM((2, *part.shape), bf16)],
            [vmem],
            (vmem, vmem),
            32,
        )(slots)
        keep.append(kept)
        received.append(lax.ppermute(send, "xline", [(x, x ^ 1) for x in range(N_X)]))
    result = jax.ShapeDtypeStruct((SAMPLES // N_IN, 4, count), jnp.float32)
    scratch = [pltpu.VMEM((96, 4, count), jnp.float32), dma]
    own = call(
        functools.partial(filter_kernel, True), "crossline_own", result, scratch, [vmem] * 3, hbm, 16
    )(matrix, *keep)
    return call(
        functools.partial(filter_kernel, False),
        "crossline_received",
        result,
        scratch,
        [vmem] * 3 + [hbm],
        hbm,
        16,
        {3: 0},
    )(matrix, *received, own)


def solution(mesh):
    split = P(("inline", "xline"))
    placed = (P(("inline", "xline"), None), P(("inline", "xline"), None), split, P(), P(), P())
    return jax.shard_map(
        shards, mesh=mesh, in_specs=placed, out_specs=P("inline", "xline", None), check_vma=False
    )
```
